256 devices in a mesh: req: 32 (over z_lo, x, core), tp: 8 (over y, z_hi).
Axes of the slice: x: 4, y: 4, z: 8 (z_hi: 2, z_lo: 4; z = z_hi * 4 + z_lo), core: 2. Of those that a mesh axis runs over, the one named last changes fastest.
Arguments:
- queries: bfloat16 [32768, 8192], P('req', 'tp'), may hold values from -6 to 6
- new_kv: bfloat16 [32768, 2048], P('req', 'tp'), may hold values from -6 to 6
- pool_kv: bfloat16 [512, 64, 2048], P(('req', 'tp')), may hold values from -6 to 6
- slot_request: int32 [64], P('req'), may hold values from 0 to 1, as said below
- prefix_ids: int32 [64, 16], P('req'), may hold values from 0 to 511, as said below
- prefix_count: int32 [64], P('req'), may hold values from 12 to 16
- block_row: int32 [512], replicated, may hold values from 0 to 511, as said below
Outputs:
- attended: bfloat16 [32768, 8192], P('req', 'tp')
The draws below stay inside these ranges and needn't reach their ends.
Inputs may be any that keep to these rules, and one draw needn't show every extreme that they name: `slot_request`: within one index of req the 2 values never fall. `prefix_ids`: no block repeats within a request. The live prefix blocks of the 2 requests of one index of req, taken together, include at most 2 distinct blocks whose rows lie on the devices of any one index of req; some draw reaches 2. `block_row`: A permutation; row g lies on device g // 2 of the joined axes req+tp.
All inputs are finite; a program needn't handle non-finite values.
Results may differ from the reference program's by a relative error of at most 0.0049.
Values may be sent and summed in bfloat16 or wider, within the bound.
No kernel may reach another device: no remote copies, remote signals or barrier semaphores. Data moves between devices by JAX's collectives and lax.ppermute only.
A program may use at most 64 MiB of HBM per device.

```python
import math
import jax
import jax.numpy as jnp
from jax import lax

HD = 128
KVH = 8
HQ = 64
SLOTS = 2
REQ_DEV = 2
PREF = 16
PB = 64
TOK_DEV = 1024
TOKENS = 32768
REQUESTS = 64
POOL = 512
GROUP_ROWS = 16
N_REQ = 32


def layout(key):
    block_perm = jax.random.permutation(jax.random.fold_in(key, 11), POOL).astype(jnp.int32)
    row_block = jnp.argsort(block_perm).astype(jnp.int32)
    pair_count = REQ_DEV * PREF // 2
    device_keys = jax.random.split(jax.random.fold_in(key, 12), N_REQ)
    groups = jax.vmap(lambda subkey: jax.random.permutation(subkey, N_REQ)[:pair_count])(device_keys)
    first_row = jax.random.randint(jax.random.fold_in(key, 13), (N_REQ, pair_count), 0, GROUP_ROWS)
    offset = jax.random.randint(jax.random.fold_in(key, 14), (N_REQ, pair_count), 1, GROUP_ROWS)
    second = (first_row + offset) % GROUP_ROWS
    within = jnp.stack([first_row, second], axis=-1).reshape(N_REQ, 2 * pair_count)
    stored = (jnp.repeat(groups, 2, axis=1) * GROUP_ROWS + within).reshape(REQUESTS, PREF)
    order_keys = jax.random.split(jax.random.fold_in(key, 15), REQUESTS)
    orders = jax.vmap(lambda subkey: jax.random.permutation(subkey, PREF))(order_keys)
    stored = jnp.take_along_axis(stored, orders, axis=1)
    return (block_perm, row_block[stored].astype(jnp.int32))


def draw_block_row(key, part):
    return layout(key)[0]


def draw_prefix_ids(key, part):
    return layout(key)[1]


def draw_prefix_count(key, part):
    key = jax.random.fold_in(key, 3)
    counts = jax.random.randint(key, (REQUESTS,), 3 * PREF // 4, PREF + 1)
    return counts.at[0].set(PREF).astype(jnp.int32)


def draw_slot_request(key, part):
    key = jax.random.fold_in(key, 4)
    owners = jax.random.randint(key, (N_REQ, SLOTS), 0, REQ_DEV)
    return jnp.sort(owners, axis=1).reshape(N_REQ * SLOTS).astype(jnp.int32)


def draw_queries(key, part):
    key = jax.random.fold_in(key, 5)
    values = jax.random.truncated_normal(key, -6.0, 6.0, (TOKENS, HQ * HD), jnp.float32)
    return values.astype(jnp.bfloat16)


def draw_new_kv(key, part):
    key = jax.random.fold_in(key, 6)
    values = jax.random.truncated_normal(key, -6.0, 6.0, (TOKENS, KVH, 2, HD), jnp.float32)
    return values.reshape(TOKENS, KVH * 2 * HD).astype(jnp.bfloat16)


def steps_of(own_key, shape, cuts, smallest, top_value):
    def one(position, shards_of):
        draws = jax.random.uniform(jax.random.fold_in(jax.random.fold_in(own_key, 6), position), (shards_of,), jnp.float32, smallest / len(cuts), top_value / len(cuts))
        return jnp.repeat(jnp.exp(draws), shape[position] // shards_of).reshape((-1,) + (1,) * (len(shape) - position - 1))

    factor_of = one(*cuts[0])
    for cut in cuts[1:]:
        factor_of = factor_of * one(*cut)
    return factor_of


def bell_draw(stream_key, extent, spread, bound, cuts=(), kind=jnp.bfloat16):
    level = steps_of(stream_key, extent, cuts, -0.22, 0.18) if cuts else 1.0
    values = jax.random.normal(stream_key, extent, jnp.float32) * spread * level
    return jnp.minimum(jnp.maximum(values, -bound), bound).astype(kind)


def setup_inputs(seed: int = 0) -> dict:
    key_list = jax.random.split(jax.random.key(seed), 8)
    queries = draw_queries(jax.random.fold_in(key_list[7], 71), 0)
    new_kv = draw_new_kv(jax.random.fold_in(key_list[7], 71), 0)
    pool_kv = bell_draw(key_list[2], (POOL, PB, 2 * KVH * HD), 1.0, 6.0, ((0, 256),))
    slot_request = draw_slot_request(jax.random.fold_in(key_list[7], 71), 0)
    prefix_ids = draw_prefix_ids(jax.random.fold_in(key_list[7], 71), 0)
    prefix_count = draw_prefix_count(jax.random.fold_in(key_list[7], 71), 0)
    block_row = draw_block_row(jax.random.fold_in(key_list[7], 71), 0)
    return {"queries": queries, "new_kv": new_kv, "pool_kv": pool_kv, "slot_request": slot_request, "prefix_ids": prefix_ids, "prefix_count": prefix_count, "block_row": block_row}


def lookup(indices, table_values):
    positions = jnp.arange(table_values.shape[0], dtype=jnp.int32)
    return lax.optimization_barrier(jnp.sum(jnp.where(indices[..., None] == positions, table_values, 0), axis=-1)).astype(jnp.int32)

def attend(queries, new_kv, prefix_kv, slot_request, prefix_count):
    slot_total = slot_request.shape[0]
    span_len = queries.shape[0] // slot_total
    head_count = queries.shape[1] // HD
    kv_heads = new_kv.shape[1] // (2 * HD)
    group_size = head_count // kv_heads
    score_scale = 1.0 / math.sqrt(HD)
    fresh_kv = new_kv.reshape(slot_total * span_len, kv_heads, 2, HD)
    cached = prefix_kv.reshape(REQ_DEV, PREF * PB, kv_heads, 2, HD)
    cached_live = (jnp.arange(PREF * PB, dtype=jnp.int32) // PB)[None, :] < prefix_count[:, None]
    token_owner = jnp.repeat(slot_request, span_len)
    pieces = []
    for slot_index in range(slot_total):
        owner_req = slot_request[slot_index]
        key_count = (slot_index + 1) * span_len
        key_index = jnp.arange(key_count, dtype=jnp.int32)
        query_index = slot_index * span_len + jnp.arange(span_len, dtype=jnp.int32)
        fresh_live = (token_owner[:key_count] == owner_req)[None, :] & (key_index[None, :] <= query_index[:, None])
        prefix_live = jnp.broadcast_to(cached_live[owner_req][None, :], (span_len, PREF * PB))
        live_mask = jnp.concatenate([prefix_live, fresh_live], axis=1)
        key_values = jnp.concatenate([cached[owner_req], fresh_kv[:key_count]], axis=0)
        query_block = queries[slot_index * span_len:(slot_index + 1) * span_len].reshape(span_len, head_count, HD)

        def one_head(head_index):
            query_head = lax.dynamic_index_in_dim(query_block, head_index, 1, keepdims=False)
            head_pair = lax.dynamic_index_in_dim(key_values, head_index // group_size, 1, keepdims=False)
            scores = jnp.dot(query_head, head_pair[:, 0].T, preferred_element_type=jnp.float32) * score_scale
            scores = jnp.where(live_mask, scores, -jnp.inf)
            row_max = lax.optimization_barrier(jnp.max(scores, axis=1, keepdims=True))
            exponent = jnp.exp(scores - row_max)
            weights = (exponent / lax.optimization_barrier(jnp.sum(exponent, axis=1, keepdims=True))).astype(jnp.bfloat16)
            return jnp.dot(weights, head_pair[:, 1], preferred_element_type=jnp.float32).astype(jnp.bfloat16)
        heads_out = lax.map(one_head, jnp.arange(head_count, dtype=jnp.int32))
        pieces.append(jnp.transpose(heads_out, (1, 0, 2)).reshape(span_len, head_count * HD))
    return jnp.concatenate(pieces, axis=0)

def reference(queries, new_kv, pool_kv, slot_request, prefix_ids, prefix_count, block_row):

    def per_device(device_index):
        query_rows = lax.dynamic_slice_in_dim(queries, device_index * TOK_DEV, TOK_DEV, 0)
        fresh_rows = lax.dynamic_slice_in_dim(new_kv, device_index * TOK_DEV, TOK_DEV, 0)
        slot_owner = lax.dynamic_slice_in_dim(slot_request, device_index * SLOTS, SLOTS, 0)
        block_ids = lax.dynamic_slice_in_dim(prefix_ids, device_index * REQ_DEV, REQ_DEV, 0)
        live_counts = lax.dynamic_slice_in_dim(prefix_count, device_index * REQ_DEV, REQ_DEV, 0)
        block_rows = lookup(block_ids, block_row)
        prefix_kv = pool_kv[block_rows].reshape(REQ_DEV, PREF * PB, 2 * KVH * HD)
        return attend(query_rows, fresh_rows, prefix_kv, slot_owner, live_counts)
    results = lax.map(per_device, jnp.arange(N_REQ, dtype=jnp.int32))
    return results.reshape(TOKENS, HQ * HD)
```

```python
import functools
import math

import jax
import jax.numpy as jnp
from jax import lax
from jax.experimental import pallas as pl
from jax.experimental.pallas import tpu as pltpu
from jax.sharding import PartitionSpec as P

HD = 128
REQ_DEV = 2
PREF = 16
PB = 64
SLOT_CAP = 2
MIN_LIVE = 12
ROW_TILE = 256
EXP_SCALE = math.log2(math.e) / math.sqrt(HD)
MASKED = -1e30


def pick_blocks(wanted, group_store):
    count = wanted.shape[0]

    def kernel(wanted_ref, store_ref, out_ref, sems):
        def copy(i):
            return pltpu.make_async_copy(store_ref.at[wanted_ref[i]], out_ref.at[i], sems.at[i])

        def start(i, carry):
            copy(i).start()
            return carry

        def finish(i, carry):
            copy(i).wait()
            return carry

        lax.fori_loop(0, count, start, 0)
        lax.fori_loop(0, count, finish, 0)

    return pl.pallas_call(
        kernel,
        grid_spec=pltpu.PrefetchScalarGridSpec(
            num_scalar_prefetch=1,
            grid=(1,),
            in_specs=[pl.BlockSpec(memory_space=pl.ANY)],
            out_specs=pl.BlockSpec(memory_space=pl.ANY),
            scratch_shapes=[pltpu.SemaphoreType.DMA((count,))],
        ),
        out_shape=jax.ShapeDtypeStruct((count,) + group_store.shape[1:], group_store.dtype),
        name="pick_blocks",
    )(wanted, group_store)


def scores_of(query_tile, keys):
    return lax.dot_general(
        query_tile, keys, (((1,), (1,)), ((), ())), preferred_element_type=jnp.float32
    )


def fresh_attention(queries, new_kv, slot_request):
    rows, width = queries.shape
    heads = width // HD
    span = rows // slot_request.shape[0]

    def kernel(owner_ref, q_ref, kv_ref, acc_ref, stat_ref, v_ext):
        @pl.when(pl.program_id(0) == 0)
        def _():
            v_ext[:, :HD] = kv_ref[:, HD:]
            v_ext[:, HD:] = jnp.ones((rows, HD), v_ext.dtype)

        same = owner_ref[0] == owner_ref[1]
        lane = lax.broadcasted_iota(jnp.int32, (ROW_TILE, HD), 1)
        for first in range(0, rows, ROW_TILE):
            last = first + ROW_TILE
            s = scores_of(q_ref[first:last, :], kv_ref[:last, :HD])
            key = lax.broadcasted_iota(jnp.int32, s.shape, 1)
            row = first + lax.broadcasted_iota(jnp.int32, s.shape, 0)
            own = (first // span) * span
            lowest = jnp.where(same, 0, own)
            s = jnp.where((key <= row) & (key >= lowest), s, MASKED)
            top = jnp.max(s, axis=1, keepdims=True)
            p = jnp.exp2((s - top) * EXP_SCALE).astype(jnp.bfloat16)
            o = jnp.dot(p, v_ext[:last, :], preferred_element_type=jnp.float32)
            acc_ref[first:last, :] = o[:, :HD]
            stat_ref[first:last, :] = jnp.where(lane < HD // 2, top, o[:, HD:])

    return pl.pallas_call(
        kernel,
        grid_spec=pltpu.PrefetchScalarGridSpec(
            num_scalar_prefetch=1,
            grid=(heads,),
            in_specs=[
                pl.BlockSpec((rows, HD), lambda h, owner: (0, h)),
                pl.BlockSpec((rows, 2 * HD), lambda h, owner: (0, 0)),
            ],
            out_specs=[
                pl.BlockSpec((rows, HD), lambda h, owner: (0, h)),
                pl.BlockSpec((rows, HD), lambda h, owner: (0, h)),
            ],
            scratch_shapes=[pltpu.VMEM((rows, 2 * HD), jnp.bfloat16)],
        ),
        out_shape=[
            jax.ShapeDtypeStruct((rows, width), jnp.float32),
            jax.ShapeDtypeStruct((rows, width), jnp.float32),
        ],
        compiler_params=pltpu.CompilerParams(vmem_limit_bytes=48 * 1024 * 1024),
        cost_estimate=pl.CostEstimate(
            flops=4 * rows * rows * width, bytes_accessed=12 * rows * width, transcendentals=rows * rows * heads
        ),
        name="fresh_attention",
    )(slot_request, queries, new_kv)


def prefix_attention(queries, received, acc, stat, slot_request, places, prefix_count):
    rows, width = queries.shape
    heads = width // HD
    slots = slot_request.shape[0]
    span = rows // slots
    keys = PREF * PB
    sure = MIN_LIVE * PB

    def kernel(owner_ref, place_ref, count_ref, q_ref, recv_ref, acc_ref, stat_ref, out_ref, k_scr, v_scr, sems):
        def copies(r, p):
            place = place_ref[r * PREF + p]
            dst = pl.ds(pl.multiple_of(p * PB, PB), PB)
            return (
                pltpu.make_async_copy(
                    recv_ref.at[place, :, pl.ds(0, HD)], k_scr.at[r, dst, :], sems.at[r, p, 0]
                ),
                pltpu.make_async_copy(
                    recv_ref.at[place, :, pl.ds(HD, HD)], v_scr.at[r, dst, pl.ds(0, HD)], sems.at[r, p, 1]
                ),
            )

        @pl.when(pl.program_id(0) == 0)
        def _():
            for r in range(REQ_DEV):
                def start(p, carry):
                    for c in copies(r, p):
                        c.start()
                    return carry

                lax.fori_loop(0, PREF, start, 0)
            v_scr[:, :, HD:] = jnp.ones((REQ_DEV, keys, HD), v_scr.dtype)
            for r in range(REQ_DEV):
                def finish(p, carry):
                    for c in copies(r, p):
                        c.wait()
                    return carry

                lax.fori_loop(0, PREF, finish, 0)

        for slot in range(slots):
            owner = owner_ref[slot]
            live = count_ref[owner] * PB
            for first in range(slot * span, (slot + 1) * span, ROW_TILE):
                tile = pl.ds(first, ROW_TILE)
                q = q_ref[tile, :]
                s = scores_of(q, k_scr[owner])
                key = sure + lax.broadcasted_iota(jnp.int32, (ROW_TILE, keys - sure), 1)
                s = jnp.concatenate([s[:, :sure], jnp.where(key < live, s[:, sure:], MASKED)], axis=1)
                old_top = stat_ref[tile, 0:1]
                top = jnp.maximum(old_top, jnp.max(s, axis=1, keepdims=True))
                p = jnp.exp2((s - top) * EXP_SCALE).astype(jnp.bfloat16)
                o = jnp.dot(p, v_scr[owner], preferred_element_type=jnp.float32)
                keep = jnp.exp2((old_top - top) * EXP_SCALE)
                total = stat_ref[tile, HD - 1 : HD] * keep + o[:, HD:]
                out_ref[tile, :] = ((acc_ref[tile, :] * keep + o[:, :HD]) / total).astype(out_ref.dtype)

    column = pl.BlockSpec((rows, HD), lambda h, *_: (0, h))
    return pl.pallas_call(
        kernel,
        grid_spec=pltpu.PrefetchScalarGridSpec(
            num_scalar_prefetch=3,
            grid=(heads,),
            in_specs=[column, pl.BlockSpec(memory_space=pl.ANY), column, column],
            out_specs=column,
            scratch_shapes=[
                pltpu.VMEM((REQ_DEV, keys, HD), jnp.bfloat16),
                pltpu.VMEM((REQ_DEV, keys, 2 * HD), jnp.bfloat16),
                pltpu.SemaphoreType.DMA((REQ_DEV, PREF, 2)),
            ],
        ),
        out_shape=jax.ShapeDtypeStruct((rows, width), jnp.bfloat16),
        compiler_params=pltpu.CompilerParams(vmem_limit_bytes=48 * 1024 * 1024),
        cost_estimate=pl.CostEstimate(
            flops=4 * rows * keys * width, bytes_accessed=12 * rows * width, transcendentals=rows * keys * heads
        ),
        name="prefix_attention",
    )(slot_request, places, prefix_count, queries, received, acc, stat)


def wanted_blocks(prefix_ids, prefix_count, block_row, groups, group_rows):
    known = jnp.arange(block_row.shape[0], dtype=jnp.int32)
    rows = jnp.sum(jnp.where(prefix_ids.reshape(-1)[:, None] == known, block_row, 0), axis=-1)
    live = (jnp.arange(PREF, dtype=jnp.int32)[None, :] < prefix_count[:, None]).reshape(-1)
    group, within = rows // group_rows, rows % group_rows
    member = live[None, :] & (group[None, :] == jnp.arange(groups, dtype=jnp.int32)[:, None])
    low = jnp.min(jnp.where(member, within[None, :], group_rows), axis=1)
    high = jnp.max(jnp.where(member, within[None, :], 0), axis=1)
    wanted = jnp.stack([jnp.minimum(low, high), high], axis=1)
    is_high = jnp.any(member & (within[None, :] > low[:, None]), axis=0)
    places = jnp.where(live, SLOT_CAP * group + is_high.astype(jnp.int32), 0)
    return wanted, places


def on_device(queries, new_kv, pool_kv, slot_request, prefix_ids, prefix_count, block_row):
    tp_count = lax.axis_size("tp")
    groups = lax.axis_size("req")
    pool_local = pool_kv.shape[0]
    head_width = pool_kv.shape[2] // tp_count
    group_rows = tp_count * pool_local
    wanted, places = wanted_blocks(prefix_ids, prefix_count, block_row, groups, group_rows)
    asked = lax.all_to_all(wanted, "req", split_axis=0, concat_axis=0, tiled=True)
    by_head = pool_kv.reshape(pool_local, PB, tp_count, head_width).transpose(2, 0, 1, 3)
    group_store = lax.all_to_all(by_head, "tp", split_axis=0, concat_axis=0, tiled=True)
    group_store = group_store.reshape(group_rows, PB, head_width)
    to_send = pick_blocks(asked.reshape(-1), group_store)
    received = lax.all_to_all(to_send, "req", split_axis=0, concat_axis=0, tiled=True)
    acc, stat = fresh_attention(queries, new_kv, slot_request)
    return prefix_attention(queries, received, acc, stat, slot_request, places, prefix_count)


def solution(mesh):
    return jax.shard_map(
        on_device,
        mesh=mesh,
        in_specs=(
            P("req", "tp"),
            P("req", "tp"),
            P(("req", "tp"), None, None),
            P("req"),
            P("req", None),
            P("req"),
            P(),
        ),
        out_specs=P("req", "tp"),
        check_vma=False,
    )
```

```python
import functools
import math

import jax
import jax.numpy as jnp
from jax import lax
from jax.experimental import pallas as pl
from jax.experimental.pallas import tpu as pltpu
from jax.sharding import PartitionSpec as P

HD = 128
REQ_DEV = 2
PREF = 16
PB = 64
SLOT_CAP = 2
MIN_LIVE = 12
PICK_STEP = 16
ROW_TILE = 256
EXP_SCALE = math.log2(math.e) / math.sqrt(HD)
MASKED = -1e30


def pick_blocks(wanted, me, group_store):
    groups = wanted.shape[0] // SLOT_CAP
    block_shape = group_store.shape[1:]

    def kernel(wanted_ref, me_ref, store_ref, out_ref):
        first = pl.program_id(0) * PICK_STEP
        for i in range(PICK_STEP):
            for j in range(SLOT_CAP):
                at = ((first + i) ^ me_ref[0]) * SLOT_CAP + j
                out_ref[SLOT_CAP * i + j] = store_ref[wanted_ref[at]]

    return pl.pallas_call(
        kernel,
        grid_spec=pltpu.PrefetchScalarGridSpec(
            num_scalar_prefetch=2,
            grid=(groups // PICK_STEP,),
            in_specs=[pl.BlockSpec(group_store.shape, lambda i, *_: (0, 0, 0))],
            out_specs=pl.BlockSpec((SLOT_CAP * PICK_STEP,) + block_shape, lambda i, *_: (i, 0, 0)),
        ),
        out_shape=jax.ShapeDtypeStruct((SLOT_CAP * groups,) + block_shape, group_store.dtype),
        name="pick_blocks",
    )(wanted, me, group_store)


def scores_of(query_tile, keys):
    return lax.dot_general(
        query_tile, keys, (((1,), (1,)), ((), ())), preferred_element_type=jnp.float32
    )


def fresh_attention(queries, new_kv, slot_request):
    rows, width = queries.shape
    heads = width // HD
    span = rows // slot_request.shape[0]

    def kernel(owner_ref, q_ref, kv_ref, acc_ref, stat_ref, v_ext):
        @pl.when(pl.program_id(0) == 0)
        def _():
            v_ext[:, :HD] = kv_ref[:, HD:]
            v_ext[:, HD:] = jnp.ones((rows, HD), v_ext.dtype)

        same = owner_ref[0] == owner_ref[1]
        lane = lax.broadcasted_iota(jnp.int32, (ROW_TILE, HD), 1)
        for first in range(0, rows, ROW_TILE):
            last = first + ROW_TILE
            s = scores_of(q_ref[first:last, :], kv_ref[:last, :HD])
            key = lax.broadcasted_iota(jnp.int32, s.shape, 1)
            row = first + lax.broadcasted_iota(jnp.int32, s.shape, 0)
            own = (first // span) * span
            lowest = jnp.where(same, 0, own)
            s = jnp.where((key <= row) & (key >= lowest), s, MASKED)
            top = jnp.max(s, axis=1, keepdims=True)
            p = jnp.exp2((s - top) * EXP_SCALE).astype(jnp.bfloat16)
            o = jnp.dot(p, v_ext[:last, :], preferred_element_type=jnp.float32)
            acc_ref[first:last, :] = o[:, :HD]
            stat_ref[first:last, :] = jnp.where(lane < HD // 2, top, o[:, HD:])

    return pl.pallas_call(
        kernel,
        grid_spec=pltpu.PrefetchScalarGridSpec(
            num_scalar_prefetch=1,
            grid=(heads,),
            in_specs=[
                pl.BlockSpec((rows, HD), lambda h, owner: (0, h)),
                pl.BlockSpec((rows, 2 * HD), lambda h, owner: (0, 0)),
            ],
            out_specs=[
                pl.BlockSpec((rows, HD), lambda h, owner: (0, h)),
                pl.BlockSpec((rows, HD), lambda h, owner: (0, h)),
            ],
            scratch_shapes=[pltpu.VMEM((rows, 2 * HD), jnp.bfloat16)],
        ),
        out_shape=[
            jax.ShapeDtypeStruct((rows, width), jnp.float32),
            jax.ShapeDtypeStruct((rows, width), jnp.float32),
        ],
        compiler_params=pltpu.CompilerParams(vmem_limit_bytes=48 * 1024 * 1024),
        cost_estimate=pl.CostEstimate(
            flops=4 * rows * rows * width, bytes_accessed=12 * rows * width, transcendentals=rows * rows * heads
        ),
        name="fresh_attention",
    )(slot_request, queries, new_kv)


def prefix_attention(queries, received, acc, stat, slot_request, places, prefix_count):
    rows, width = queries.shape
    heads = width // HD
    slots = slot_request.shape[0]
    span = rows // slots
    keys = PREF * PB
    sure = MIN_LIVE * PB

    def kernel(owner_ref, place_ref, count_ref, q_ref, recv_ref, acc_ref, stat_ref, out_ref, k_scr, v_scr, sems):
        def copies(r, p):
            place = place_ref[r * PREF + p]
            dst = pl.ds(pl.multiple_of(p * PB, PB), PB)
            return (
                pltpu.make_async_copy(
                    recv_ref.at[place, :, pl.ds(0, HD)], k_scr.at[r, dst, :], sems.at[r, p, 0]
                ),
                pltpu.make_async_copy(
                    recv_ref.at[place, :, pl.ds(HD, HD)], v_scr.at[r, dst, pl.ds(0, HD)], sems.at[r, p, 1]
                ),
            )

        @pl.when(pl.program_id(0) == 0)
        def _():
            for r in range(REQ_DEV):
                def start(p, carry):
                    for c in copies(r, p):
                        c.start()
                    return carry

                lax.fori_loop(0, PREF, start, 0)
            v_scr[:, :, HD:] = jnp.ones((REQ_DEV, keys, HD), v_scr.dtype)
            for r in range(REQ_DEV):
                def finish(p, carry):
                    for c in copies(r, p):
                        c.wait()
                    return carry

                lax.fori_loop(0, PREF, finish, 0)

        for slot in range(slots):
            owner = owner_ref[slot]
            live = count_ref[owner] * PB
            for first in range(slot * span, (slot + 1) * span, ROW_TILE):
                tile = pl.ds(first, ROW_TILE)
                q = q_ref[tile, :]
                s = scores_of(q, k_scr[owner])
                key = sure + lax.broadcasted_iota(jnp.int32, (ROW_TILE, keys - sure), 1)
                s = jnp.concatenate([s[:, :sure], jnp.where(key < live, s[:, sure:], MASKED)], axis=1)
                old_top = stat_ref[tile, 0:1]
                top = jnp.maximum(old_top, jnp.max(s, axis=1, keepdims=True))
                p = jnp.exp2((s - top) * EXP_SCALE).astype(jnp.bfloat16)
                o = jnp.dot(p, v_scr[owner], preferred_element_type=jnp.float32)
                keep = jnp.exp2((old_top - top) * EXP_SCALE)
                total = stat_ref[tile, HD - 1 : HD] * keep + o[:, HD:]
                out_ref[tile, :] = ((acc_ref[tile, :] * keep + o[:, :HD]) / total).astype(out_ref.dtype)

    column = pl.BlockSpec((rows, HD), lambda h, *_: (0, h))
    return pl.pallas_call(
        kernel,
        grid_spec=pltpu.PrefetchScalarGridSpec(
            num_scalar_prefetch=3,
            grid=(heads,),
            in_specs=[column, pl.BlockSpec(memory_space=pl.ANY), column, column],
            out_specs=column,
            scratch_shapes=[
                pltpu.VMEM((REQ_DEV, keys, HD), jnp.bfloat16),
                pltpu.VMEM((REQ_DEV, keys, 2 * HD), jnp.bfloat16),
                pltpu.SemaphoreType.DMA((REQ_DEV, PREF, 2)),
            ],
        ),
        out_shape=jax.ShapeDtypeStruct((rows, width), jnp.bfloat16),
        compiler_params=pltpu.CompilerParams(vmem_limit_bytes=48 * 1024 * 1024),
        cost_estimate=pl.CostEstimate(
            flops=4 * rows * keys * width, bytes_accessed=12 * rows * width, transcendentals=rows * keys * heads
        ),
        name="prefix_attention",
    )(slot_request, places, prefix_count, queries, received, acc, stat)


def used_rows(prefix_ids, prefix_count, block_row):
    known = jnp.arange(block_row.shape[0], dtype=jnp.int32)
    ids = prefix_ids.reshape(-1)
    rows = jnp.sum(jnp.where(ids[:, None] == known, block_row, 0), axis=-1)
    live = (jnp.arange(PREF, dtype=jnp.int32)[None, :] < prefix_count[:, None]).reshape(-1)
    return jnp.where(live, rows, -1)


def share_over_req(values):
    groups = lax.axis_size("req")
    known = values[None, :]
    for steps in ((1,), (2, 4, 6), (8, 16, 24)):
        parts = [lax.ppermute(known, "req", [(d, d ^ step) for d in range(groups)]) for step in steps]
        known = jnp.concatenate([known] + parts, axis=0)
    return known


def low_high(rows, first_row, group_rows):
    within = rows - first_row
    member = (within >= 0) & (within < group_rows)
    low = jnp.min(jnp.where(member, within, group_rows), axis=-1)
    high = jnp.max(jnp.where(member, within, 0), axis=-1)
    return jnp.minimum(low, high), high


def on_device(queries, new_kv, pool_kv, slot_request, prefix_ids, prefix_count, block_row):
    tp_count = lax.axis_size("tp")
    groups = lax.axis_size("req")
    me = lax.axis_index("req").astype(jnp.int32)
    pool_local = pool_kv.shape[0]
    head_width = pool_kv.shape[2] // tp_count
    group_rows = tp_count * pool_local
    rows = used_rows(prefix_ids, prefix_count, block_row)
    low, high = low_high(share_over_req(rows), me * group_rows, group_rows)
    wanted = jnp.stack([low, high], axis=1).reshape(-1)
    by_head = pool_kv.reshape(pool_local, PB, tp_count, head_width).transpose(2, 0, 1, 3)
    group_store = lax.all_to_all(by_head, "tp", split_axis=0, concat_axis=0, tiled=True)
    group_store = group_store.reshape(group_rows, PB, head_width)
    to_send = pick_blocks(wanted, me[None], group_store)
    received = lax.all_to_all(to_send, "req", split_axis=0, concat_axis=0, tiled=True)
    same_group = rows[:, None] // group_rows == rows[None, :] // group_rows
    is_high = jnp.any(same_group & (rows[None, :] < rows[:, None]) & (rows[None, :] >= 0), axis=1)
    places = jnp.where(rows >= 0, SLOT_CAP * (rows // group_rows) + is_high.astype(jnp.int32), 0)
    acc, stat = fresh_attention(queries, new_kv, slot_request)
    return prefix_attention(queries, received, acc, stat, slot_request, places, prefix_count)


def solution(mesh):
    return jax.shard_map(
        on_device,
        mesh=mesh,
        in_specs=(
            P("req", "tp"),
            P("req", "tp"),
            P(("req", "tp"), None, None),
            P("req"),
            P("req", None),
            P("req"),
            P(),
        ),
        out_specs=P("req", "tp"),
        check_vma=False,
    )
```

```python
import functools
import math

import jax
import jax.numpy as jnp
from jax import lax
from jax.experimental import pallas as pl
from jax.experimental.pallas import tpu as pltpu
from jax.sharding import PartitionSpec as P

HD = 128
REQ_DEV = 2
PREF = 16
PB = 64
SLOT_CAP = 2
MIN_LIVE = 12
PICK_STEP = 16
ROW_TILE = 256
EXP_SCALE = math.log2(math.e) / math.sqrt(HD)
MASKED = -1e30
HEAD_STEP = 2
KEY_BOUND = 6.0
EXP2_LIMIT = 112.0
FRESH_VMEM_LIMIT = 51712 * 1024
PREFIX_VMEM_LIMIT = 51712 * 1024
PICK_VMEM_LIMIT = 8 * 1024 * 1024


def pick_blocks(wanted, me, group_store):
    groups = wanted.shape[0] // SLOT_CAP
    block_shape = group_store.shape[1:]

    def kernel(wanted_ref, me_ref, store_ref, out_ref):
        first = pl.program_id(0) * PICK_STEP
        for i in range(PICK_STEP):
            for j in range(SLOT_CAP):
                at = ((first + i) ^ me_ref[0]) * SLOT_CAP + j
                out_ref[SLOT_CAP * i + j] = store_ref[wanted_ref[at]]

    return pl.pallas_call(
        kernel,
        grid_spec=pltpu.PrefetchScalarGridSpec(
            num_scalar_prefetch=2,
            grid=(groups // PICK_STEP,),
            in_specs=[pl.BlockSpec(memory_space=pltpu.VMEM)],
            out_specs=pl.BlockSpec((SLOT_CAP * PICK_STEP,) + block_shape, lambda i, *_: (i, 0, 0)),
        ),
        out_shape=jax.ShapeDtypeStruct((SLOT_CAP * groups,) + block_shape, group_store.dtype),
        compiler_params=pltpu.CompilerParams(vmem_limit_bytes=PICK_VMEM_LIMIT),
        name="pick_blocks",
    )(wanted, me, group_store)


def scores_of(query_tile, keys):
    return lax.dot_general(
        query_tile, keys, (((1,), (1,)), ((), ())), preferred_element_type=jnp.float32
    )


def fresh_attention(queries, new_kv, slot_request):
    rows, width = queries.shape
    steps = width // HD // HEAD_STEP
    span = rows // slot_request.shape[0]

    def kernel(owner_ref, q_ref, kv_ref, acc_ref, stat_ref, excess_ref, v_ext):
        @pl.when(pl.program_id(0) == 0)
        def _():
            v_ext[:, :HD] = kv_ref[:, HD:]
            v_ext[:, HD:] = jnp.ones((rows, HD), v_ext.dtype)

        same = owner_ref[0] == owner_ref[1]
        lane = lax.broadcasted_iota(jnp.int32, (ROW_TILE, HD), 1)
        excess = None
        for first in range(0, rows, ROW_TILE):
            last = first + ROW_TILE
            stat = jnp.zeros((ROW_TILE, HD), jnp.float32)
            for part in range(HEAD_STEP):
                column = slice(part * HD, (part + 1) * HD)
                q = q_ref[first:last, column]
                s = scores_of(q, kv_ref[:last, :HD])
                key = lax.broadcasted_iota(jnp.int32, s.shape, 1)
                row = first + lax.broadcasted_iota(jnp.int32, s.shape, 0)
                own = (first // span) * span
                lowest = jnp.where(same, 0, own)
                s = jnp.where((key <= row) & (key >= lowest), s, MASKED)
                top = jnp.max(s, axis=1, keepdims=True)
                p = jnp.exp2((s - top) * EXP_SCALE).astype(jnp.bfloat16)
                o = jnp.dot(p, v_ext[:last, :], preferred_element_type=jnp.float32)
                acc_ref[first:last, column] = o[:, :HD]
                stat = jnp.where(lane == 2 * part, top, jnp.where(lane == 2 * part + 1, o[:, HD:], stat))
                reach = KEY_BOUND * jnp.sum(jnp.abs(q.astype(jnp.float32)), axis=1, keepdims=True)
                over = jnp.max((reach - top) * EXP_SCALE)
                excess = over if excess is None else jnp.maximum(excess, over)
            stat_ref[0, first:last, :] = stat
        excess_ref[pl.program_id(0)] = excess

    return pl.pallas_call(
        kernel,
        grid_spec=pltpu.PrefetchScalarGridSpec(
            num_scalar_prefetch=1,
            grid=(steps,),
            in_specs=[
                pl.BlockSpec((rows, HEAD_STEP * HD), lambda h, owner: (0, h)),
                pl.BlockSpec((rows, 2 * HD), lambda h, owner: (0, 0)),
            ],
            out_specs=[
                pl.BlockSpec((rows, HEAD_STEP * HD), lambda h, owner: (0, h)),
                pl.BlockSpec((1, rows, HD), lambda h, owner: (h, 0, 0)),
                pl.BlockSpec(memory_space=pltpu.SMEM),
            ],
            scratch_shapes=[pltpu.VMEM((rows, 2 * HD), jnp.bfloat16)],
        ),
        out_shape=[
            jax.ShapeDtypeStruct((rows, width), jnp.float32),
            jax.ShapeDtypeStruct((steps, rows, HD), jnp.float32),
            jax.ShapeDtypeStruct((steps,), jnp.float32),
        ],
        compiler_params=pltpu.CompilerParams(vmem_limit_bytes=FRESH_VMEM_LIMIT),
        cost_estimate=pl.CostEstimate(
            flops=4 * rows * rows * width, bytes_accessed=12 * rows * width, transcendentals=rows * rows * width // HD
        ),
        name="fresh_attention",
    )(slot_request, queries, new_kv)


def prefix_attention(queries, received, acc, stat, excess, slot_request, places, prefix_count):
    rows, width = queries.shape
    steps = width // HD // HEAD_STEP
    step_width = HEAD_STEP * HD
    slots = slot_request.shape[0]
    span = rows // slots
    keys = PREF * PB
    sure = MIN_LIVE * PB

    def kernel(
        owner_ref, place_ref, count_ref, excess_ref, q_any, recv_ref, acc_any, stat_any, out_any,
        k_scr, v_scr, q_scr, acc_scr, stat_scr, out_scr, in_sem, out_sem,
    ):
        def gather(i, carry):
            request, to = i // PREF, pl.ds(pl.multiple_of((i % PREF) * PB, PB), PB)
            block = recv_ref[place_ref[i]]
            k_scr[request, to, :] = block[:, :HD]
            v_scr[request, to, :HD] = block[:, HD:]
            return carry

        def in_copies(step):
            column = pl.ds(pl.multiple_of(step * step_width, step_width), step_width)
            return (
                pltpu.make_async_copy(q_any.at[:, column], q_scr.at[step], in_sem.at[step, 0]),
                pltpu.make_async_copy(acc_any.at[:, column], acc_scr.at[step], in_sem.at[step, 1]),
                pltpu.make_async_copy(stat_any.at[step], stat_scr.at[step], in_sem.at[step, 2]),
            )

        def out_copy(step):
            column = pl.ds(pl.multiple_of(step * step_width, step_width), step_width)
            return pltpu.make_async_copy(out_scr.at[step], out_any.at[:, column], out_sem.at[step])

        for copy in in_copies(0):
            copy.start()
        v_scr[:, :, HD:] = jnp.ones((REQ_DEV, keys, HD), v_scr.dtype)
        lax.fori_loop(0, REQ_DEV * PREF, gather, 0, unroll=4)

        def attend(step, with_maximum):
            for part in range(HEAD_STEP):
                column = slice(part * HD, (part + 1) * HD)
                for slot in range(slots):
                    owner = owner_ref[slot]
                    live = count_ref[owner] * PB
                    for first in range(slot * span, (slot + 1) * span, ROW_TILE):
                        tile = slice(first, first + ROW_TILE)
                        s = scores_of(q_scr[step, tile, column], k_scr[owner])
                        key = sure + lax.broadcasted_iota(jnp.int32, (ROW_TILE, keys - sure), 1)
                        s = jnp.concatenate([s[:, :sure], jnp.where(key < live, s[:, sure:], MASKED)], axis=1)
                        top = stat_scr[step, tile, 2 * part : 2 * part + 1]
                        total = stat_scr[step, tile, 2 * part + 1 : 2 * part + 2]
                        total_acc = acc_scr[step, tile, column]
                        if with_maximum:
                            old_top = top
                            top = jnp.maximum(old_top, jnp.max(s, axis=1, keepdims=True))
                            keep = jnp.exp2((old_top - top) * EXP_SCALE)
                            total, total_acc = total * keep, total_acc * keep
                        p = jnp.exp2((s - top) * EXP_SCALE).astype(jnp.bfloat16)
                        o = jnp.dot(p, v_scr[owner], preferred_element_type=jnp.float32)
                        result = (total_acc + o[:, :HD]) / (total + o[:, HD:])
                        out_scr[step, tile, column] = result.astype(out_scr.dtype)

        def one_step(step, carry):
            @pl.when(step + 1 < steps)
            def _():
                for copy in in_copies(step + 1):
                    copy.start()

            for copy in in_copies(step):
                copy.wait()
            bounded = excess_ref[step] < EXP2_LIMIT

            @pl.when(bounded)
            def _():
                attend(step, False)

            @pl.when(jnp.logical_not(bounded))
            def _():
                attend(step, True)

            out_copy(step).start()
            return carry

        lax.fori_loop(0, steps, one_step, 0)
        for step in range(steps):
            out_copy(step).wait()

    smem, anywhere = pl.BlockSpec(memory_space=pltpu.SMEM), pl.BlockSpec(memory_space=pl.ANY)
    return pl.pallas_call(
        kernel,
        in_specs=[smem] * 4 + [anywhere, pl.BlockSpec(memory_space=pltpu.VMEM), anywhere, anywhere],
        out_specs=anywhere,
        scratch_shapes=[
            pltpu.VMEM((REQ_DEV, keys, HD), jnp.bfloat16),
            pltpu.VMEM((REQ_DEV, keys, 2 * HD), jnp.bfloat16),
            pltpu.VMEM((steps, rows, step_width), jnp.bfloat16),
            pltpu.VMEM((steps, rows, step_width), jnp.float32),
            pltpu.VMEM((steps, rows, HD), jnp.float32),
            pltpu.VMEM((steps, rows, step_width), jnp.bfloat16),
            pltpu.SemaphoreType.DMA((steps, 3)),
            pltpu.SemaphoreType.DMA((steps,)),
        ],
        out_shape=jax.ShapeDtypeStruct((rows, width), jnp.bfloat16),
        compiler_params=pltpu.CompilerParams(vmem_limit_bytes=PREFIX_VMEM_LIMIT),
        cost_estimate=pl.CostEstimate(
            flops=4 * rows * keys * width, bytes_accessed=12 * rows * width, transcendentals=rows * keys * width // HD
        ),
        name="prefix_attention",
    )(slot_request, places, prefix_count, excess, queries, received, acc, stat)


def used_rows(prefix_ids, prefix_count, block_row):
    known = jnp.arange(block_row.shape[0], dtype=jnp.int32)
    ids = prefix_ids.reshape(-1)
    rows = jnp.sum(jnp.where(ids[:, None] == known, block_row, 0), axis=-1)
    live = (jnp.arange(PREF, dtype=jnp.int32)[None, :] < prefix_count[:, None]).reshape(-1)
    return jnp.where(live, rows, -1)


def share_over_req(values):
    groups = lax.axis_size("req")
    known = values[None, :]
    for steps in ((1,), (2, 4, 6), (8, 16, 24)):
        parts = [lax.ppermute(known, "req", [(d, d ^ step) for d in range(groups)]) for step in steps]
        known = jnp.concatenate([known] + parts, axis=0)
    return known


def low_high(rows, first_row, group_rows):
    within = rows - first_row
    member = (within >= 0) & (within < group_rows)
    low = jnp.min(jnp.where(member, within, group_rows), axis=-1)
    high = jnp.max(jnp.where(member, within, 0), axis=-1)
    return jnp.minimum(low, high), high


def on_device(queries, new_kv, pool_kv, slot_request, prefix_ids, prefix_count, block_row):
    tp_count = lax.axis_size("tp")
    groups = lax.axis_size("req")
    me = lax.axis_index("req").astype(jnp.int32)
    pool_local = pool_kv.shape[0]
    head_width = pool_kv.shape[2] // tp_count
    group_rows = tp_count * pool_local
    rows = used_rows(prefix_ids, prefix_count, block_row)
    low, high = low_high(share_over_req(rows), me * group_rows, group_rows)
    wanted = jnp.stack([low, high], axis=1).reshape(-1)
    by_head = pool_kv.reshape(pool_local, PB, tp_count, head_width).transpose(2, 0, 1, 3)
    group_store = lax.all_to_all(by_head, "tp", split_axis=0, concat_axis=0, tiled=True)
    group_store = group_store.reshape(group_rows, PB, head_width)
    to_send = pick_blocks(wanted, me[None], group_store)
    received = lax.all_to_all(to_send, "req", split_axis=0, concat_axis=0, tiled=True)
    same_group = rows[:, None] // group_rows == rows[None, :] // group_rows
    is_high = jnp.any(same_group & (rows[None, :] < rows[:, None]) & (rows[None, :] >= 0), axis=1)
    places = jnp.where(rows >= 0, SLOT_CAP * (rows // group_rows) + is_high.astype(jnp.int32), 0)
    acc, stat, excess = fresh_attention(queries, new_kv, slot_request)
    return prefix_attention(queries, received, acc, stat, excess, slot_request, places, prefix_count)


def solution(mesh):
    return jax.shard_map(
        on_device,
        mesh=mesh,
        in_specs=(
            P("req", "tp"),
            P("req", "tp"),
            P(("req", "tp"), None, None),
            P("req"),
            P("req", None),
            P("req"),
            P(),
        ),
        out_specs=P("req", "tp"),
        check_vma=False,
    )
```

```python
import functools
import math

import jax
import jax.numpy as jnp
from jax import lax
from jax.experimental import pallas as pl
from jax.experimental.pallas import tpu as pltpu
from jax.sharding import PartitionSpec as P

HD = 128
REQ_DEV = 2
PREF = 16
PB = 64
SLOT_CAP = 2
MIN_LIVE = 12
PICK_STEP = 4
ROW_TILE = 256
EXP_SCALE = math.log2(math.e) / math.sqrt(HD)
MASKED = -1e30
HEAD_STEP = 2
KEY_BOUND = 6.0
EXP2_LIMIT = 112.0
FRESH_VMEM_LIMIT = 51712 * 1024
PREFIX_VMEM_LIMIT = 51712 * 1024
PICK_VMEM_LIMIT = 8 * 1024 * 1024


def pick_blocks(wanted, me, group_store):
    count = wanted.shape[0]
    block_shape = group_store.shape[1:]
    step_blocks = SLOT_CAP * PICK_STEP
    steps = count // step_blocks

    def kernel(wanted_ref, me_ref, store_ref, out_any, picked, sems):
        def send(step):
            blocks = pl.ds(step * step_blocks, step_blocks)
            return pltpu.make_async_copy(picked.at[blocks], out_any.at[blocks], sems.at[step])

        for step in range(steps):
            for i in range(step * PICK_STEP, (step + 1) * PICK_STEP):
                for j in range(SLOT_CAP):
                    picked[SLOT_CAP * i + j] = store_ref[wanted_ref[(i ^ me_ref[0]) * SLOT_CAP + j]]
            send(step).start()
        for step in range(steps):
            send(step).wait()

    smem = pl.BlockSpec(memory_space=pltpu.SMEM)
    return pl.pallas_call(
        kernel,
        in_specs=[smem, smem, pl.BlockSpec(memory_space=pltpu.VMEM)],
        out_specs=pl.BlockSpec(memory_space=pl.ANY),
        scratch_shapes=[
            pltpu.VMEM((count,) + block_shape, group_store.dtype),
            pltpu.SemaphoreType.DMA((steps,)),
        ],
        out_shape=jax.ShapeDtypeStruct((count,) + block_shape, group_store.dtype),
        compiler_params=pltpu.CompilerParams(vmem_limit_bytes=PICK_VMEM_LIMIT),
        name="pick_blocks",
    )(wanted, me, group_store)


def scores_of(query_tile, keys):
    return lax.dot_general(
        query_tile, keys, (((1,), (1,)), ((), ())), preferred_element_type=jnp.float32
    )


def fresh_attention(queries, new_kv, slot_request):
    rows, width = queries.shape
    steps = width // HD // HEAD_STEP
    span = rows // slot_request.shape[0]

    def kernel(owner_ref, q_ref, kv_ref, acc_ref, stat_ref, excess_ref, v_ext):
        @pl.when(pl.program_id(0) == 0)
        def _():
            v_ext[:, :HD] = kv_ref[:, HD:]
            v_ext[:, HD:] = jnp.ones((rows, HD), v_ext.dtype)

        same = owner_ref[0] == owner_ref[1]
        lane = lax.broadcasted_iota(jnp.int32, (ROW_TILE, HD), 1)
        excess = None
        for first in range(0, rows, ROW_TILE):
            last = first + ROW_TILE
            stat = jnp.zeros((ROW_TILE, HD), jnp.float32)
            for part in range(HEAD_STEP):
                column = slice(part * HD, (part + 1) * HD)
                q = q_ref[first:last, column]
                s = scores_of(q, kv_ref[:last, :HD])
                key = lax.broadcasted_iota(jnp.int32, s.shape, 1)
                row = first + lax.broadcasted_iota(jnp.int32, s.shape, 0)
                own = (first // span) * span
                lowest = jnp.where(same, 0, own)
                s = jnp.where((key <= row) & (key >= lowest), s, MASKED)
                top = jnp.max(s, axis=1, keepdims=True)
                p = jnp.exp2((s - top) * EXP_SCALE).astype(jnp.bfloat16)
                o = jnp.dot(p, v_ext[:last, :], preferred_element_type=jnp.float32)
                acc_ref[first:last, column] = o[:, :HD]
                stat = jnp.where(lane == 2 * part, top, jnp.where(lane == 2 * part + 1, o[:, HD:], stat))
                reach = KEY_BOUND * jnp.sum(jnp.abs(q.astype(jnp.float32)), axis=1, keepdims=True)
                over = jnp.max((reach - top) * EXP_SCALE)
                excess = over if excess is None else jnp.maximum(excess, over)
            stat_ref[0, first:last, :] = stat
        excess_ref[pl.program_id(0)] = excess

    return pl.pallas_call(
        kernel,
        grid_spec=pltpu.PrefetchScalarGridSpec(
            num_scalar_prefetch=1,
            grid=(steps,),
            in_specs=[
                pl.BlockSpec((rows, HEAD_STEP * HD), lambda h, owner: (0, h)),
                pl.BlockSpec((rows, 2 * HD), lambda h, owner: (0, 0)),
            ],
            out_specs=[
                pl.BlockSpec((rows, HEAD_STEP * HD), lambda h, owner: (0, h)),
                pl.BlockSpec((1, rows, HD), lambda h, owner: (h, 0, 0)),
                pl.BlockSpec(memory_space=pltpu.SMEM),
            ],
            scratch_shapes=[pltpu.VMEM((rows, 2 * HD), jnp.bfloat16)],
        ),
        out_shape=[
            jax.ShapeDtypeStruct((rows, width), jnp.float32),
            jax.ShapeDtypeStruct((steps, rows, HD), jnp.float32),
            jax.ShapeDtypeStruct((steps,), jnp.float32),
        ],
        compiler_params=pltpu.CompilerParams(vmem_limit_bytes=FRESH_VMEM_LIMIT),
        cost_estimate=pl.CostEstimate(
            flops=4 * rows * rows * width, bytes_accessed=12 * rows * width, transcendentals=rows * rows * width // HD
        ),
        name="fresh_attention",
    )(slot_request, queries, new_kv)


def prefix_attention(queries, received, acc, stat, excess, slot_request, places, prefix_count):
    rows, width = queries.shape
    steps = width // HD // HEAD_STEP
    step_width = HEAD_STEP * HD
    slots = slot_request.shape[0]
    span = rows // slots
    keys = PREF * PB
    sure = MIN_LIVE * PB

    def kernel(
        owner_ref, place_ref, count_ref, excess_ref, q_any, recv_any, acc_any, stat_any, out_any,
        kv_scr, v_scr, q_scr, acc_scr, stat_scr, out_scr, kv_sem, in_sem, out_sem,
    ):
        def kv_copy(i):
            request, to = i // PREF, pl.ds(pl.multiple_of((i % PREF) * PB, PB), PB)
            return pltpu.make_async_copy(recv_any.at[place_ref[i]], kv_scr.at[request, to, :], kv_sem.at[i])

        def start_kv(i, carry):
            kv_copy(i).start()
            return carry

        def wait_kv(i, carry):
            kv_copy(i).wait()
            return carry

        def in_copies(step):
            column = pl.ds(pl.multiple_of(step * step_width, step_width), step_width)
            return (
                pltpu.make_async_copy(q_any.at[:, column], q_scr.at[step], in_sem.at[step, 0]),
                pltpu.make_async_copy(acc_any.at[:, column], acc_scr.at[step], in_sem.at[step, 1]),
                pltpu.make_async_copy(stat_any.at[step], stat_scr.at[step], in_sem.at[step, 2]),
            )

        def out_copy(step):
            column = pl.ds(pl.multiple_of(step * step_width, step_width), step_width)
            return pltpu.make_async_copy(out_scr.at[step], out_any.at[:, column], out_sem.at[step])

        lax.fori_loop(0, REQ_DEV * PREF, start_kv, 0, unroll=8)
        for copy in in_copies(0):
            copy.start()
        v_scr[:, :, HD:] = jnp.ones((REQ_DEV, keys, HD), v_scr.dtype)
        lax.fori_loop(0, REQ_DEV * PREF, wait_kv, 0, unroll=8)
        v_scr[:, :, :HD] = kv_scr[:, :, HD:]

        def attend(step, with_maximum):
            for part in range(HEAD_STEP):
                column = slice(part * HD, (part + 1) * HD)
                for slot in range(slots):
                    owner = owner_ref[slot]
                    live = count_ref[owner] * PB
                    for first in range(slot * span, (slot + 1) * span, ROW_TILE):
                        tile = slice(first, first + ROW_TILE)
                        s = scores_of(q_scr[step, tile, column], kv_scr[owner, :, :HD])
                        key = sure + lax.broadcasted_iota(jnp.int32, (ROW_TILE, keys - sure), 1)
                        s = jnp.concatenate([s[:, :sure], jnp.where(key < live, s[:, sure:], MASKED)], axis=1)
                        top = stat_scr[step, tile, 2 * part : 2 * part + 1]
                        total = stat_scr[step, tile, 2 * part + 1 : 2 * part + 2]
                        total_acc = acc_scr[step, tile, column]
                        if with_maximum:
                            old_top = top
                            top = jnp.maximum(old_top, jnp.max(s, axis=1, keepdims=True))
                            keep = jnp.exp2((old_top - top) * EXP_SCALE)
                            total, total_acc = total * keep, total_acc * keep
                        p = jnp.exp2((s - top) * EXP_SCALE).astype(jnp.bfloat16)
                        o = jnp.dot(p, v_scr[owner], preferred_element_type=jnp.float32)
                        result = (total_acc + o[:, :HD]) / (total + o[:, HD:])
                        out_scr[step, tile, column] = result.astype(out_scr.dtype)

        def one_step(step, carry):
            @pl.when(step + 1 < steps)
            def _():
                for copy in in_copies(step + 1):
                    copy.start()

            for copy in in_copies(step):
                copy.wait()
            bounded = excess_ref[step] < EXP2_LIMIT

            @pl.when(bounded)
            def _():
                attend(step, False)

            @pl.when(jnp.logical_not(bounded))
            def _():
                attend(step, True)

            out_copy(step).start()
            return carry

        lax.fori_loop(0, steps, one_step, 0)
        for step in range(steps):
            out_copy(step).wait()

    smem, anywhere = pl.BlockSpec(memory_space=pltpu.SMEM), pl.BlockSpec(memory_space=pl.ANY)
    return pl.pallas_call(
        kernel,
        in_specs=[smem] * 4 + [anywhere] * 4,
        out_specs=anywhere,
        scratch_shapes=[
            pltpu.VMEM((REQ_DEV, keys, 2 * HD), jnp.bfloat16),
            pltpu.VMEM((REQ_DEV, keys, 2 * HD), jnp.bfloat16),
            pltpu.VMEM((steps, rows, step_width), jnp.bfloat16),
            pltpu.VMEM((steps, rows, step_width), jnp.float32),
            pltpu.VMEM((steps, rows, HD), jnp.float32),
            pltpu.VMEM((steps, rows, step_width), jnp.bfloat16),
            pltpu.SemaphoreType.DMA((REQ_DEV * PREF,)),
            pltpu.SemaphoreType.DMA((steps, 3)),
            pltpu.SemaphoreType.DMA((steps,)),
        ],
        out_shape=jax.ShapeDtypeStruct((rows, width), jnp.bfloat16),
        compiler_params=pltpu.CompilerParams(vmem_limit_bytes=PREFIX_VMEM_LIMIT),
        cost_estimate=pl.CostEstimate(
            flops=4 * rows * keys * width, bytes_accessed=12 * rows * width, transcendentals=rows * keys * width // HD
        ),
        name="prefix_attention",
    )(slot_request, places, prefix_count, excess, queries, received, acc, stat)


def used_rows(prefix_ids, prefix_count, block_row):
    known = jnp.arange(block_row.shape[0], dtype=jnp.int32)
    ids = prefix_ids.reshape(-1)
    rows = jnp.sum(jnp.where(ids[:, None] == known, block_row, 0), axis=-1)
    live = (jnp.arange(PREF, dtype=jnp.int32)[None, :] < prefix_count[:, None]).reshape(-1)
    return jnp.where(live, rows, -1)


def share_over_req(values):
    groups = lax.axis_size("req")
    known = values[None, :]
    for steps in ((1,), (2, 4, 6), (8, 16, 24)):
        parts = [lax.ppermute(known, "req", [(d, d ^ step) for d in range(groups)]) for step in steps]
        known = jnp.concatenate([known] + parts, axis=0)
    return known


def low_high(rows, first_row, group_rows):
    within = rows - first_row
    member = (within >= 0) & (within < group_rows)
    low = jnp.min(jnp.where(member, within, group_rows), axis=-1)
    high = jnp.max(jnp.where(member, within, 0), axis=-1)
    return jnp.minimum(low, high), high


def on_device(queries, new_kv, pool_kv, slot_request, prefix_ids, prefix_count, block_row):
    tp_count = lax.axis_size("tp")
    groups = lax.axis_size("req")
    me = lax.axis_index("req").astype(jnp.int32)
    pool_local = pool_kv.shape[0]
    head_width = pool_kv.shape[2] // tp_count
    group_rows = tp_count * pool_local
    rows = used_rows(prefix_ids, prefix_count, block_row)
    low, high = low_high(share_over_req(rows), me * group_rows, group_rows)
    wanted = jnp.stack([low, high], axis=1).reshape(-1)
    by_head = pool_kv.reshape(pool_local, PB, tp_count, head_width).transpose(2, 0, 1, 3)
    group_store = lax.all_to_all(by_head, "tp", split_axis=0, concat_axis=0, tiled=True)
    group_store = group_store.reshape(group_rows, PB, head_width)
    to_send = pick_blocks(wanted, me[None], group_store)
    received = lax.all_to_all(to_send, "req", split_axis=0, concat_axis=0, tiled=True)
    same_group = rows[:, None] // group_rows == rows[None, :] // group_rows
    is_high = jnp.any(same_group & (rows[None, :] < rows[:, None]) & (rows[None, :] >= 0), axis=1)
    places = jnp.where(rows >= 0, SLOT_CAP * (rows // group_rows) + is_high.astype(jnp.int32), 0)
    acc, stat, excess = fresh_attention(queries, new_kv, slot_request)
    return prefix_attention(queries, received, acc, stat, excess, slot_request, places, prefix_count)


def solution(mesh):
    return jax.shard_map(
        on_device,
        mesh=mesh,
        in_specs=(
            P("req", "tp"),
            P("req", "tp"),
            P(("req", "tp"), None, None),
            P("req"),
            P("req", None),
            P("req"),
            P(),
        ),
        out_specs=P("req", "tp"),
        check_vma=False,
    )
```

```python
import functools
import math

import jax
import jax.numpy as jnp
from jax import lax
from jax.experimental import pallas as pl
from jax.experimental.pallas import tpu as pltpu
from jax.sharding import PartitionSpec as P

HD = 128
REQ_DEV = 2
PREF = 16
PB = 64
SLOT_CAP = 2
MIN_LIVE = 12
PICK_STEP = 4
ROW_TILE = 256
EXP_SCALE = math.log2(math.e) / math.sqrt(HD)
MASKED = -1e30
HEAD_STEP = 2
KEY_BOUND = 6.0
EXP2_LIMIT = 112.0
FRESH_VMEM_LIMIT = 51712 * 1024
PREFIX_VMEM_LIMIT = 51712 * 1024
PICK_VMEM_LIMIT = 8 * 1024 * 1024


def pick_blocks(wanted, me, group_store):
    count = wanted.shape[0]
    block_shape = group_store.shape[1:]
    step_blocks = SLOT_CAP * PICK_STEP
    steps = count // step_blocks

    def kernel(wanted_ref, me_ref, store_ref, out_any, picked, sems):
        def send(step):
            blocks = pl.ds(step * step_blocks, step_blocks)
            return pltpu.make_async_copy(picked.at[blocks], out_any.at[blocks], sems.at[step])

        for step in range(steps):
            for i in range(step * PICK_STEP, (step + 1) * PICK_STEP):
                for j in range(SLOT_CAP):
                    picked[SLOT_CAP * i + j] = store_ref[wanted_ref[(i ^ me_ref[0]) * SLOT_CAP + j]]
            send(step).start()
        for step in range(steps):
            send(step).wait()

    smem = pl.BlockSpec(memory_space=pltpu.SMEM)
    return pl.pallas_call(
        kernel,
        in_specs=[smem, smem, pl.BlockSpec(memory_space=pltpu.VMEM)],
        out_specs=pl.BlockSpec(memory_space=pl.ANY),
        scratch_shapes=[
            pltpu.VMEM((count,) + block_shape, group_store.dtype),
            pltpu.SemaphoreType.DMA((steps,)),
        ],
        out_shape=jax.ShapeDtypeStruct((count,) + block_shape, group_store.dtype),
        compiler_params=pltpu.CompilerParams(vmem_limit_bytes=PICK_VMEM_LIMIT),
        name="pick_blocks",
    )(wanted, me, group_store)


def scores_of(query_tile, keys):
    return lax.dot_general(
        query_tile, keys, (((1,), (1,)), ((), ())), preferred_element_type=jnp.float32
    )


def fresh_attention(queries, new_kv, slot_request):
    rows, width = queries.shape
    steps = width // HD // HEAD_STEP
    span = rows // slot_request.shape[0]

    def kernel(owner_ref, q_ref, kv_ref, acc_ref, stat_ref, excess_ref, v_ext):
        @pl.when(pl.program_id(0) == 0)
        def _():
            v_ext[:, :HD] = kv_ref[:, HD:]
            v_ext[:, HD:] = jnp.ones((rows, HD), v_ext.dtype)

        same = owner_ref[0] == owner_ref[1]
        lane = lax.broadcasted_iota(jnp.int32, (ROW_TILE, HD), 1)
        excess = None
        for first in range(0, rows, ROW_TILE):
            last = first + ROW_TILE
            stat = jnp.zeros((ROW_TILE, HD), jnp.float32)
            for part in range(HEAD_STEP):
                column = slice(part * HD, (part + 1) * HD)
                q = q_ref[first:last, column]
                s = scores_of(q, kv_ref[:last, :HD])
                key = lax.broadcasted_iota(jnp.int32, s.shape, 1)
                row = first + lax.broadcasted_iota(jnp.int32, s.shape, 0)
                own = (first // span) * span
                lowest = jnp.where(same, 0, own)
                s = jnp.where((key <= row) & (key >= lowest), s, MASKED)
                top = jnp.max(s, axis=1, keepdims=True)
                p = jnp.exp2((s - top) * EXP_SCALE).astype(jnp.bfloat16)
                o = jnp.dot(p, v_ext[:last, :], preferred_element_type=jnp.float32)
                acc_ref[first:last, column] = o[:, :HD]
                stat = jnp.where(lane == 2 * part, top, jnp.where(lane == 2 * part + 1, o[:, HD:], stat))
                reach = KEY_BOUND * jnp.sum(jnp.abs(q.astype(jnp.float32)), axis=1, keepdims=True)
                over = jnp.max((reach - top) * EXP_SCALE)
                excess = over if excess is None else jnp.maximum(excess, over)
            stat_ref[0, first:last, :] = stat
        excess_ref[pl.program_id(0)] = excess

    return pl.pallas_call(
        kernel,
        grid_spec=pltpu.PrefetchScalarGridSpec(
            num_scalar_prefetch=1,
            grid=(steps,),
            in_specs=[
                pl.BlockSpec((rows, HEAD_STEP * HD), lambda h, owner: (0, h)),
                pl.BlockSpec((rows, 2 * HD), lambda h, owner: (0, 0)),
            ],
            out_specs=[
                pl.BlockSpec((rows, HEAD_STEP * HD), lambda h, owner: (0, h)),
                pl.BlockSpec((1, rows, HD), lambda h, owner: (h, 0, 0)),
                pl.BlockSpec(memory_space=pltpu.SMEM),
            ],
            scratch_shapes=[pltpu.VMEM((rows, 2 * HD), jnp.bfloat16)],
        ),
        out_shape=[
            jax.ShapeDtypeStruct((rows, width), jnp.float32),
            jax.ShapeDtypeStruct((steps, rows, HD), jnp.float32),
            jax.ShapeDtypeStruct((steps,), jnp.float32),
        ],
        compiler_params=pltpu.CompilerParams(vmem_limit_bytes=FRESH_VMEM_LIMIT),
        cost_estimate=pl.CostEstimate(
            flops=4 * rows * rows * width, bytes_accessed=12 * rows * width, transcendentals=rows * rows * width // HD
        ),
        name="fresh_attention",
    )(slot_request, queries, new_kv)


def prefix_attention(queries, received, acc, stat, excess, slot_request, places, prefix_count):
    rows, width = queries.shape
    steps = width // HD // HEAD_STEP
    step_width = HEAD_STEP * HD
    slots = slot_request.shape[0]
    span = rows // slots
    keys = PREF * PB
    sure = MIN_LIVE * PB

    def kernel(
        owner_ref, place_ref, count_ref, excess_ref, q_ref, recv_any, acc_any, stat_any, out_any,
        kv_scr, v_scr, acc_scr, stat_scr, out_scr, kv_sem, in_sem, out_sem,
    ):
        def kv_copy(i):
            request, to = i // PREF, pl.ds(pl.multiple_of((i % PREF) * PB, PB), PB)
            return pltpu.make_async_copy(recv_any.at[place_ref[i]], kv_scr.at[request, to, :], kv_sem.at[i])

        def start_kv(i, carry):
            kv_copy(i).start()
            return carry

        def wait_kv(i, carry):
            kv_copy(i).wait()
            return carry

        def in_copies(step):
            column = pl.ds(pl.multiple_of(step * step_width, step_width), step_width)
            return (
                pltpu.make_async_copy(acc_any.at[:, column], acc_scr.at[step], in_sem.at[step, 0]),
                pltpu.make_async_copy(stat_any.at[step], stat_scr.at[step], in_sem.at[step, 1]),
            )

        def out_copy(step):
            column = pl.ds(pl.multiple_of(step * step_width, step_width), step_width)
            return pltpu.make_async_copy(out_scr.at[step], out_any.at[:, column], out_sem.at[step])

        lax.fori_loop(0, REQ_DEV * PREF, start_kv, 0, unroll=8)
        for copy in in_copies(0):
            copy.start()
        v_scr[:, :, HD:] = jnp.ones((REQ_DEV, keys, HD), v_scr.dtype)
        lax.fori_loop(0, REQ_DEV * PREF, wait_kv, 0, unroll=8)
        v_scr[:, :, :HD] = kv_scr[:, :, HD:]

        def attend(step, with_maximum):
            for part in range(HEAD_STEP):
                column = slice(part * HD, (part + 1) * HD)
                q_column = pl.ds(pl.multiple_of((step * HEAD_STEP + part) * HD, HD), HD)
                for slot in range(slots):
                    owner = owner_ref[slot]
                    live = count_ref[owner] * PB
                    for first in range(slot * span, (slot + 1) * span, ROW_TILE):
                        tile = slice(first, first + ROW_TILE)
                        s = scores_of(q_ref[tile, q_column], kv_scr[owner, :, :HD])
                        key = sure + lax.broadcasted_iota(jnp.int32, (ROW_TILE, keys - sure), 1)
                        s = jnp.concatenate([s[:, :sure], jnp.where(key < live, s[:, sure:], MASKED)], axis=1)
                        top = stat_scr[step, tile, 2 * part : 2 * part + 1]
                        total = stat_scr[step, tile, 2 * part + 1 : 2 * part + 2]
                        total_acc = acc_scr[step, tile, column]
                        if with_maximum:
                            old_top = top
                            top = jnp.maximum(old_top, jnp.max(s, axis=1, keepdims=True))
                            keep = jnp.exp2((old_top - top) * EXP_SCALE)
                            total, total_acc = total * keep, total_acc * keep
                        p = jnp.exp2((s - top) * EXP_SCALE).astype(jnp.bfloat16)
                        o = jnp.dot(p, v_scr[owner], preferred_element_type=jnp.float32)
                        result = (total_acc + o[:, :HD]) / (total + o[:, HD:])
                        out_scr[step, tile, column] = result.astype(out_scr.dtype)

        def one_step(step, carry):
            @pl.when(step + 1 < steps)
            def _():
                for copy in in_copies(step + 1):
                    copy.start()

            for copy in in_copies(step):
                copy.wait()
            bounded = excess_ref[step] < EXP2_LIMIT

            @pl.when(bounded)
            def _():
                attend(step, False)

            @pl.when(jnp.logical_not(bounded))
            def _():
                attend(step, True)

            out_copy(step).start()
            return carry

        lax.fori_loop(0, steps, one_step, 0)
        for step in range(steps):
            out_copy(step).wait()

    smem, anywhere = pl.BlockSpec(memory_space=pltpu.SMEM), pl.BlockSpec(memory_space=pl.ANY)
    return pl.pallas_call(
        kernel,
        in_specs=[smem] * 4 + [pl.BlockSpec(memory_space=pltpu.VMEM)] + [anywhere] * 3,
        out_specs=anywhere,
        scratch_shapes=[
            pltpu.VMEM((REQ_DEV, keys, 2 * HD), jnp.bfloat16),
            pltpu.VMEM((REQ_DEV, keys, 2 * HD), jnp.bfloat16),
            pltpu.VMEM((steps, rows, step_width), jnp.float32),
            pltpu.VMEM((steps, rows, HD), jnp.float32),
            pltpu.VMEM((steps, rows, step_width), jnp.bfloat16),
            pltpu.SemaphoreType.DMA((REQ_DEV * PREF,)),
            pltpu.SemaphoreType.DMA((steps, 2)),
            pltpu.SemaphoreType.DMA((steps,)),
        ],
        out_shape=jax.ShapeDtypeStruct((rows, width), jnp.bfloat16),
        compiler_params=pltpu.CompilerParams(vmem_limit_bytes=PREFIX_VMEM_LIMIT),
        cost_estimate=pl.CostEstimate(
            flops=4 * rows * keys * width, bytes_accessed=12 * rows * width, transcendentals=rows * keys * width // HD
        ),
        name="prefix_attention",
    )(slot_request, places, prefix_count, excess, queries, received, acc, stat)


def used_rows(prefix_ids, prefix_count, block_row):
    known = jnp.arange(block_row.shape[0], dtype=jnp.int32)
    ids = prefix_ids.reshape(-1)
    rows = jnp.sum(jnp.where(ids[:, None] == known, block_row, 0), axis=-1)
    live = (jnp.arange(PREF, dtype=jnp.int32)[None, :] < prefix_count[:, None]).reshape(-1)
    return jnp.where(live, rows, -1)


def share_over_req(values):
    groups = lax.axis_size("req")
    known = values[None, :]
    for steps in ((1,), (2, 4, 6), (8, 16, 24)):
        parts = [lax.ppermute(known, "req", [(d, d ^ step) for d in range(groups)]) for step in steps]
        known = jnp.concatenate([known] + parts, axis=0)
    return known


def low_high(rows, first_row, group_rows):
    within = rows - first_row
    member = (within >= 0) & (within < group_rows)
    low = jnp.min(jnp.where(member, within, group_rows), axis=-1)
    high = jnp.max(jnp.where(member, within, 0), axis=-1)
    return jnp.minimum(low, high), high


def on_device(queries, new_kv, pool_kv, slot_request, prefix_ids, prefix_count, block_row):
    tp_count = lax.axis_size("tp")
    groups = lax.axis_size("req")
    me = lax.axis_index("req").astype(jnp.int32)
    pool_local = pool_kv.shape[0]
    head_width = pool_kv.shape[2] // tp_count
    group_rows = tp_count * pool_local
    rows = used_rows(prefix_ids, prefix_count, block_row)
    low, high = low_high(share_over_req(rows), me * group_rows, group_rows)
    wanted = jnp.stack([low, high], axis=1).reshape(-1)
    by_head = pool_kv.reshape(pool_local, PB, tp_count, head_width).transpose(2, 0, 1, 3)
    group_store = lax.all_to_all(by_head, "tp", split_axis=0, concat_axis=0, tiled=True)
    group_store = group_store.reshape(group_rows, PB, head_width)
    to_send = pick_blocks(wanted, me[None], group_store)
    received = lax.all_to_all(to_send, "req", split_axis=0, concat_axis=0, tiled=True)
    same_group = rows[:, None] // group_rows == rows[None, :] // group_rows
    is_high = jnp.any(same_group & (rows[None, :] < rows[:, None]) & (rows[None, :] >= 0), axis=1)
    places = jnp.where(rows >= 0, SLOT_CAP * (rows // group_rows) + is_high.astype(jnp.int32), 0)
    acc, stat, excess = fresh_attention(queries, new_kv, slot_request)
    return prefix_attention(queries, received, acc, stat, excess, slot_request, places, prefix_count)


def solution(mesh):
    return jax.shard_map(
        on_device,
        mesh=mesh,
        in_specs=(
            P("req", "tp"),
            P("req", "tp"),
            P(("req", "tp"), None, None),
            P("req"),
            P("req", None),
            P("req"),
            P(),
        ),
        out_specs=P("req", "tp"),
        check_vma=False,
    )
```

```python
import functools
import math

import jax
import jax.numpy as jnp
from jax import lax
from jax.experimental import pallas as pl
from jax.experimental.pallas import tpu as pltpu
from jax.sharding import PartitionSpec as P

HD = 128
REQ_DEV = 2
PREF = 16
PB = 64
SLOT_CAP = 2
MIN_LIVE = 12
PICK_STEP = 4
ROW_TILE = 256
EXP_SCALE = math.log2(math.e) / math.sqrt(HD)
MASKED = -1e30
HEAD_STEP = 2
KEY_BOUND = 6.0
EXP2_LIMIT = 112.0
FRESH_VMEM_LIMIT = 51712 * 1024
PREFIX_VMEM_LIMIT = 51712 * 1024
PICK_VMEM_LIMIT = 8 * 1024 * 1024
LAY_VMEM_LIMIT = 60 * 1024 * 1024


def lay_by_head(pool_kv, head_width):
    blocks, tokens, columns = pool_kv.shape
    heads = columns // head_width

    def kernel(pool_ref, out_ref):
        for head in range(heads):
            out_ref[head, 0] = pool_ref[0, :, head * head_width : (head + 1) * head_width]

    return pl.pallas_call(
        kernel,
        grid=(blocks,),
        in_specs=[pl.BlockSpec((1, tokens, columns), lambda i: (i, 0, 0))],
        out_specs=pl.BlockSpec((heads, 1, tokens, head_width), lambda i: (0, i, 0, 0)),
        out_shape=jax.ShapeDtypeStruct((heads, blocks, tokens, head_width), pool_kv.dtype),
        compiler_params=pltpu.CompilerParams(vmem_limit_bytes=LAY_VMEM_LIMIT),
        name="lay_by_head",
    )(pool_kv)


def pick_blocks(wanted, me, group_store):
    count = wanted.shape[0]
    block_shape = group_store.shape[1:]
    step_blocks = SLOT_CAP * PICK_STEP
    steps = count // step_blocks

    def kernel(wanted_ref, me_ref, store_ref, out_any, picked, sems):
        def send(step):
            blocks = pl.ds(step * step_blocks, step_blocks)
            return pltpu.make_async_copy(picked.at[blocks], out_any.at[blocks], sems.at[step])

        for step in range(steps):
            for i in range(step * PICK_STEP, (step + 1) * PICK_STEP):
                for j in range(SLOT_CAP):
                    picked[SLOT_CAP * i + j] = store_ref[wanted_ref[(i ^ me_ref[0]) * SLOT_CAP + j]]
            send(step).start()
        for step in range(steps):
            send(step).wait()

    smem = pl.BlockSpec(memory_space=pltpu.SMEM)
    return pl.pallas_call(
        kernel,
        in_specs=[smem, smem, pl.BlockSpec(memory_space=pltpu.VMEM)],
        out_specs=pl.BlockSpec(memory_space=pl.ANY),
        scratch_shapes=[
            pltpu.VMEM((count,) + block_shape, group_store.dtype),
            pltpu.SemaphoreType.DMA((steps,)),
        ],
        out_shape=jax.ShapeDtypeStruct((count,) + block_shape, group_store.dtype),
        compiler_params=pltpu.CompilerParams(vmem_limit_bytes=PICK_VMEM_LIMIT),
        name="pick_blocks",
    )(wanted, me, group_store)


def scores_of(query_tile, keys):
    return lax.dot_general(
        query_tile, keys, (((1,), (1,)), ((), ())), preferred_element_type=jnp.float32
    )


def fresh_attention(queries, new_kv, slot_request):
    rows, width = queries.shape
    steps = width // HD // HEAD_STEP
    span = rows // slot_request.shape[0]

    def kernel(owner_ref, q_ref, kv_ref, acc_ref, stat_ref, excess_ref, v_ext):
        @pl.when(pl.program_id(0) == 0)
        def _():
            v_ext[:, :HD] = kv_ref[:, HD:]
            v_ext[:, HD:] = jnp.ones((rows, HD), v_ext.dtype)

        same = owner_ref[0] == owner_ref[1]
        lane = lax.broadcasted_iota(jnp.int32, (ROW_TILE, HD), 1)
        excess = None
        for first in range(0, rows, ROW_TILE):
            last = first + ROW_TILE
            stat = jnp.zeros((ROW_TILE, HD), jnp.float32)
            for part in range(HEAD_STEP):
                column = slice(part * HD, (part + 1) * HD)
                q = q_ref[first:last, column]
                s = scores_of(q, kv_ref[:last, :HD])
                key = lax.broadcasted_iota(jnp.int32, s.shape, 1)
                row = first + lax.broadcasted_iota(jnp.int32, s.shape, 0)
                own = (first // span) * span
                lowest = jnp.where(same, 0, own)
                s = jnp.where((key <= row) & (key >= lowest), s, MASKED)
                top = jnp.max(s, axis=1, keepdims=True)
                p = jnp.exp2((s - top) * EXP_SCALE).astype(jnp.bfloat16)
                o = jnp.dot(p, v_ext[:last, :], preferred_element_type=jnp.float32)
                acc_ref[first:last, column] = o[:, :HD]
                stat = jnp.where(lane == 2 * part, top, jnp.where(lane == 2 * part + 1, o[:, HD:], stat))
                reach = KEY_BOUND * jnp.sum(jnp.abs(q.astype(jnp.float32)), axis=1, keepdims=True)
                over = jnp.max((reach - top) * EXP_SCALE)
                excess = over if excess is None else jnp.maximum(excess, over)
            stat_ref[0, first:last, :] = stat
        excess_ref[pl.program_id(0)] = excess

    return pl.pallas_call(
        kernel,
        grid_spec=pltpu.PrefetchScalarGridSpec(
            num_scalar_prefetch=1,
            grid=(steps,),
            in_specs=[
                pl.BlockSpec((rows, HEAD_STEP * HD), lambda h, owner: (0, h)),
                pl.BlockSpec((rows, 2 * HD), lambda h, owner: (0, 0)),
            ],
            out_specs=[
                pl.BlockSpec((rows, HEAD_STEP * HD), lambda h, owner: (0, h)),
                pl.BlockSpec((1, rows, HD), lambda h, owner: (h, 0, 0)),
                pl.BlockSpec(memory_space=pltpu.SMEM),
            ],
            scratch_shapes=[pltpu.VMEM((rows, 2 * HD), jnp.bfloat16)],
        ),
        out_shape=[
            jax.ShapeDtypeStruct((rows, width), jnp.float32),
            jax.ShapeDtypeStruct((steps, rows, HD), jnp.float32),
            jax.ShapeDtypeStruct((steps,), jnp.float32),
        ],
        compiler_params=pltpu.CompilerParams(vmem_limit_bytes=FRESH_VMEM_LIMIT),
        cost_estimate=pl.CostEstimate(
            flops=4 * rows * rows * width, bytes_accessed=12 * rows * width, transcendentals=rows * rows * width // HD
        ),
        name="fresh_attention",
    )(slot_request, queries, new_kv)


def prefix_attention(queries, received, acc, stat, excess, slot_request, places, prefix_count):
    rows, width = queries.shape
    steps = width // HD // HEAD_STEP
    step_width = HEAD_STEP * HD
    slots = slot_request.shape[0]
    span = rows // slots
    keys = PREF * PB
    sure = MIN_LIVE * PB

    def kernel(
        owner_ref, place_ref, count_ref, excess_ref, q_ref, recv_any, acc_any, stat_any, out_any,
        kv_scr, v_scr, acc_scr, stat_scr, out_scr, kv_sem, in_sem, out_sem,
    ):
        def kv_copy(i):
            request, to = i // PREF, pl.ds(pl.multiple_of((i % PREF) * PB, PB), PB)
            return pltpu.make_async_copy(recv_any.at[place_ref[i]], kv_scr.at[request, to, :], kv_sem.at[i])

        def start_kv(i, carry):
            kv_copy(i).start()
            return carry

        def wait_kv(i, carry):
            kv_copy(i).wait()
            return carry

        def in_copies(step):
            column = pl.ds(pl.multiple_of(step * step_width, step_width), step_width)
            return (
                pltpu.make_async_copy(acc_any.at[:, column], acc_scr.at[step], in_sem.at[step, 0]),
                pltpu.make_async_copy(stat_any.at[step], stat_scr.at[step], in_sem.at[step, 1]),
            )

        def out_copy(step):
            column = pl.ds(pl.multiple_of(step * step_width, step_width), step_width)
            return pltpu.make_async_copy(out_scr.at[step], out_any.at[:, column], out_sem.at[step])

        lax.fori_loop(0, REQ_DEV * PREF, start_kv, 0, unroll=8)
        for copy in in_copies(0):
            copy.start()
        v_scr[:, :, HD:] = jnp.ones((REQ_DEV, keys, HD), v_scr.dtype)
        lax.fori_loop(0, REQ_DEV * PREF, wait_kv, 0, unroll=8)
        v_scr[:, :, :HD] = kv_scr[:, :, HD:]

        def attend(step, with_maximum):
            for part in range(HEAD_STEP):
                column = slice(part * HD, (part + 1) * HD)
                q_column = pl.ds(pl.multiple_of((step * HEAD_STEP + part) * HD, HD), HD)
                for slot in range(slots):
                    owner = owner_ref[slot]
                    live = count_ref[owner] * PB
                    for first in range(slot * span, (slot + 1) * span, ROW_TILE):
                        tile = slice(first, first + ROW_TILE)
                        s = scores_of(q_ref[tile, q_column], kv_scr[owner, :, :HD])
                        key = sure + lax.broadcasted_iota(jnp.int32, (ROW_TILE, keys - sure), 1)
                        s = jnp.concatenate([s[:, :sure], jnp.where(key < live, s[:, sure:], MASKED)], axis=1)
                        top = stat_scr[step, tile, 2 * part : 2 * part + 1]
                        total = stat_scr[step, tile, 2 * part + 1 : 2 * part + 2]
                        total_acc = acc_scr[step, tile, column]
                        if with_maximum:
                            old_top = top
                            top = jnp.maximum(old_top, jnp.max(s, axis=1, keepdims=True))
                            keep = jnp.exp2((old_top - top) * EXP_SCALE)
                            total, total_acc = total * keep, total_acc * keep
                        p = jnp.exp2((s - top) * EXP_SCALE).astype(jnp.bfloat16)
                        o = jnp.dot(p, v_scr[owner], preferred_element_type=jnp.float32)
                        result = (total_acc + o[:, :HD]) / (total + o[:, HD:])
                        out_scr[step, tile, column] = result.astype(out_scr.dtype)

        def one_step(step, carry):
            @pl.when(step + 1 < steps)
            def _():
                for copy in in_copies(step + 1):
                    copy.start()

            for copy in in_copies(step):
                copy.wait()
            bounded = excess_ref[step] < EXP2_LIMIT

            @pl.when(bounded)
            def _():
                attend(step, False)

            @pl.when(jnp.logical_not(bounded))
            def _():
                attend(step, True)

            out_copy(step).start()
            return carry

        lax.fori_loop(0, steps, one_step, 0)
        for step in range(steps):
            out_copy(step).wait()

    smem, anywhere = pl.BlockSpec(memory_space=pltpu.SMEM), pl.BlockSpec(memory_space=pl.ANY)
    return pl.pallas_call(
        kernel,
        in_specs=[smem] * 4 + [pl.BlockSpec(memory_space=pltpu.VMEM)] + [anywhere] * 3,
        out_specs=anywhere,
        scratch_shapes=[
            pltpu.VMEM((REQ_DEV, keys, 2 * HD), jnp.bfloat16),
            pltpu.VMEM((REQ_DEV, keys, 2 * HD), jnp.bfloat16),
            pltpu.VMEM((steps, rows, step_width), jnp.float32),
            pltpu.VMEM((steps, rows, HD), jnp.float32),
            pltpu.VMEM((steps, rows, step_width), jnp.bfloat16),
            pltpu.SemaphoreType.DMA((REQ_DEV * PREF,)),
            pltpu.SemaphoreType.DMA((steps, 2)),
            pltpu.SemaphoreType.DMA((steps,)),
        ],
        out_shape=jax.ShapeDtypeStruct((rows, width), jnp.bfloat16),
        compiler_params=pltpu.CompilerParams(vmem_limit_bytes=PREFIX_VMEM_LIMIT),
        cost_estimate=pl.CostEstimate(
            flops=4 * rows * keys * width, bytes_accessed=12 * rows * width, transcendentals=rows * keys * width // HD
        ),
        name="prefix_attention",
    )(slot_request, places, prefix_count, excess, queries, received, acc, stat)


def used_rows(prefix_ids, prefix_count, block_row):
    known = jnp.arange(block_row.shape[0], dtype=jnp.int32)
    ids = prefix_ids.reshape(-1)
    rows = jnp.sum(jnp.where(ids[:, None] == known, block_row, 0), axis=-1)
    live = (jnp.arange(PREF, dtype=jnp.int32)[None, :] < prefix_count[:, None]).reshape(-1)
    return jnp.where(live, rows, -1)


def share_over_req(values):
    groups = lax.axis_size("req")
    known = values[None, :]
    for steps in ((1,), (2, 4, 6), (8, 16, 24)):
        parts = [lax.ppermute(known, "req", [(d, d ^ step) for d in range(groups)]) for step in steps]
        known = jnp.concatenate([known] + parts, axis=0)
    return known


def low_high(rows, first_row, group_rows):
    within = rows - first_row
    member = (within >= 0) & (within < group_rows)
    low = jnp.min(jnp.where(member, within, group_rows), axis=-1)
    high = jnp.max(jnp.where(member, within, 0), axis=-1)
    return jnp.minimum(low, high), high


def on_device(queries, new_kv, pool_kv, slot_request, prefix_ids, prefix_count, block_row):
    tp_count = lax.axis_size("tp")
    groups = lax.axis_size("req")
    me = lax.axis_index("req").astype(jnp.int32)
    pool_local = pool_kv.shape[0]
    head_width = pool_kv.shape[2] // tp_count
    group_rows = tp_count * pool_local
    rows = used_rows(prefix_ids, prefix_count, block_row)
    low, high = low_high(share_over_req(rows), me * group_rows, group_rows)
    wanted = jnp.stack([low, high], axis=1).reshape(-1)
    by_head = lay_by_head(pool_kv, head_width)
    group_store = lax.all_to_all(by_head, "tp", split_axis=0, concat_axis=0, tiled=True)
    group_store = group_store.reshape(group_rows, PB, head_width)
    to_send = pick_blocks(wanted, me[None], group_store)
    received = lax.all_to_all(to_send, "req", split_axis=0, concat_axis=0, tiled=True)
    same_group = rows[:, None] // group_rows == rows[None, :] // group_rows
    is_high = jnp.any(same_group & (rows[None, :] < rows[:, None]) & (rows[None, :] >= 0), axis=1)
    places = jnp.where(rows >= 0, SLOT_CAP * (rows // group_rows) + is_high.astype(jnp.int32), 0)
    acc, stat, excess = fresh_attention(queries, new_kv, slot_request)
    return prefix_attention(queries, received, acc, stat, excess, slot_request, places, prefix_count)


def solution(mesh):
    return jax.shard_map(
        on_device,
        mesh=mesh,
        in_specs=(
            P("req", "tp"),
            P("req", "tp"),
            P(("req", "tp"), None, None),
            P("req"),
            P("req", None),
            P("req"),
            P(),
        ),
        out_specs=P("req", "tp"),
        check_vma=False,
    )
```

```python
import functools
import math

import jax
import jax.numpy as jnp
from jax import lax
from jax.experimental import pallas as pl
from jax.experimental.pallas import tpu as pltpu
from jax.sharding import PartitionSpec as P

HD = 128
REQ_DEV = 2
PREF = 16
PB = 64
SLOT_CAP = 2
MIN_LIVE = 12
PICK_STEP = 8
ROW_TILE = 256
EXP_SCALE = math.log2(math.e) / math.sqrt(HD)
MASKED = -1e30
HEAD_STEP = 2
KEY_BOUND = 6.0
EXP2_LIMIT = 112.0
FRESH_VMEM_LIMIT = 51712 * 1024
PREFIX_VMEM_LIMIT = 51712 * 1024
PICK_VMEM_LIMIT = 8 * 1024 * 1024
LAY_VMEM_LIMIT = 60 * 1024 * 1024


def lay_by_head(pool_kv, head_width):
    blocks, tokens, columns = pool_kv.shape
    heads = columns // head_width

    def kernel(pool_ref, out_ref):
        for head in range(heads):
            out_ref[head, 0] = pool_ref[0, :, head * head_width : (head + 1) * head_width]

    return pl.pallas_call(
        kernel,
        grid=(blocks,),
        in_specs=[pl.BlockSpec((1, tokens, columns), lambda i: (i, 0, 0))],
        out_specs=pl.BlockSpec((heads, 1, tokens, head_width), lambda i: (0, i, 0, 0)),
        out_shape=jax.ShapeDtypeStruct((heads, blocks, tokens, head_width), pool_kv.dtype),
        compiler_params=pltpu.CompilerParams(vmem_limit_bytes=LAY_VMEM_LIMIT),
        name="lay_by_head",
    )(pool_kv)


def pick_blocks(wanted, me, group_store):
    count = wanted.shape[0]
    block_shape = group_store.shape[1:]
    step_blocks = SLOT_CAP * PICK_STEP
    steps = count // step_blocks

    def kernel(wanted_ref, me_ref, store_ref, out_any, picked, sems):
        def send(step):
            blocks = pl.ds(step * step_blocks, step_blocks)
            return pltpu.make_async_copy(picked.at[blocks], out_any.at[blocks], sems.at[step])

        for step in range(steps):
            for i in range(step * PICK_STEP, (step + 1) * PICK_STEP):
                for j in range(SLOT_CAP):
                    picked[SLOT_CAP * i + j] = store_ref[wanted_ref[(i ^ me_ref[0]) * SLOT_CAP + j]]
            send(step).start()
        for step in range(steps):
            send(step).wait()

    smem = pl.BlockSpec(memory_space=pltpu.SMEM)
    return pl.pallas_call(
        kernel,
        in_specs=[smem, smem, pl.BlockSpec(memory_space=pltpu.VMEM)],
        out_specs=pl.BlockSpec(memory_space=pl.ANY),
        scratch_shapes=[
            pltpu.VMEM((count,) + block_shape, group_store.dtype),
            pltpu.SemaphoreType.DMA((steps,)),
        ],
        out_shape=jax.ShapeDtypeStruct((count,) + block_shape, group_store.dtype),
        compiler_params=pltpu.CompilerParams(vmem_limit_bytes=PICK_VMEM_LIMIT),
        name="pick_blocks",
    )(wanted, me, group_store)


def scores_of(query_tile, keys):
    return lax.dot_general(
        query_tile, keys, (((1,), (1,)), ((), ())), preferred_element_type=jnp.float32
    )


def fresh_attention(queries, new_kv, slot_request):
    rows, width = queries.shape
    steps = width // HD // HEAD_STEP
    span = rows // slot_request.shape[0]

    def kernel(owner_ref, q_ref, kv_ref, acc_ref, stat_ref, excess_ref, v_ext):
        @pl.when(pl.program_id(0) == 0)
        def _():
            v_ext[:, :HD] = kv_ref[:, HD:]
            v_ext[:, HD:] = jnp.ones((rows, HD), v_ext.dtype)

        same = owner_ref[0] == owner_ref[1]
        lane = lax.broadcasted_iota(jnp.int32, (ROW_TILE, HD), 1)
        excess = None
        for first in range(0, rows, ROW_TILE):
            last = first + ROW_TILE
            stat = jnp.zeros((ROW_TILE, HD), jnp.float32)
            for part in range(HEAD_STEP):
                column = slice(part * HD, (part + 1) * HD)
                q = q_ref[first:last, column]
                s = scores_of(q, kv_ref[:last, :HD])
                key = lax.broadcasted_iota(jnp.int32, s.shape, 1)
                row = first + lax.broadcasted_iota(jnp.int32, s.shape, 0)
                own = (first // span) * span
                lowest = jnp.where(same, 0, own)
                s = jnp.where((key <= row) & (key >= lowest), s, MASKED)
                top = jnp.max(s, axis=1, keepdims=True)
                p = jnp.exp2((s - top) * EXP_SCALE).astype(jnp.bfloat16)
                o = jnp.dot(p, v_ext[:last, :], preferred_element_type=jnp.float32)
                acc_ref[first:last, column] = o[:, :HD]
                stat = jnp.where(lane == 2 * part, top, jnp.where(lane == 2 * part + 1, o[:, HD:], stat))
                reach = KEY_BOUND * jnp.sum(jnp.abs(q.astype(jnp.float32)), axis=1, keepdims=True)
                over = jnp.max((reach - top) * EXP_SCALE)
                excess = over if excess is None else jnp.maximum(excess, over)
            stat_ref[0, first:last, :] = stat
        excess_ref[pl.program_id(0)] = excess

    return pl.pallas_call(
        kernel,
        grid_spec=pltpu.PrefetchScalarGridSpec(
            num_scalar_prefetch=1,
            grid=(steps,),
            in_specs=[
                pl.BlockSpec((rows, HEAD_STEP * HD), lambda h, owner: (0, h)),
                pl.BlockSpec((rows, 2 * HD), lambda h, owner: (0, 0)),
            ],
            out_specs=[
                pl.BlockSpec((rows, HEAD_STEP * HD), lambda h, owner: (0, h)),
                pl.BlockSpec((1, rows, HD), lambda h, owner: (h, 0, 0)),
                pl.BlockSpec(memory_space=pltpu.SMEM),
            ],
            scratch_shapes=[pltpu.VMEM((rows, 2 * HD), jnp.bfloat16)],
        ),
        out_shape=[
            jax.ShapeDtypeStruct((rows, width), jnp.float32),
            jax.ShapeDtypeStruct((steps, rows, HD), jnp.float32),
            jax.ShapeDtypeStruct((steps,), jnp.float32),
        ],
        compiler_params=pltpu.CompilerParams(vmem_limit_bytes=FRESH_VMEM_LIMIT),
        cost_estimate=pl.CostEstimate(
            flops=4 * rows * rows * width, bytes_accessed=12 * rows * width, transcendentals=rows * rows * width // HD
        ),
        name="fresh_attention",
    )(slot_request, queries, new_kv)


def prefix_attention(queries, received, acc, stat, excess, slot_request, places, prefix_count):
    rows, width = queries.shape
    steps = width // HD // HEAD_STEP
    step_width = HEAD_STEP * HD
    slots = slot_request.shape[0]
    span = rows // slots
    keys = PREF * PB
    sure = MIN_LIVE * PB

    def kernel(
        owner_ref, place_ref, count_ref, excess_ref, q_ref, recv_any, acc_any, stat_any, out_any,
        kv_scr, v_scr, acc_scr, stat_scr, out_scr, kv_sem, in_sem, out_sem,
    ):
        def kv_copy(i):
            request, to = i // PREF, pl.ds(pl.multiple_of((i % PREF) * PB, PB), PB)
            return pltpu.make_async_copy(recv_any.at[place_ref[i]], kv_scr.at[request, to, :], kv_sem.at[i])

        def start_kv(i, carry):
            kv_copy(i).start()
            return carry

        def wait_kv(i, carry):
            kv_copy(i).wait()
            return carry

        def in_copies(step):
            column = pl.ds(pl.multiple_of(step * step_width, step_width), step_width)
            return (
                pltpu.make_async_copy(acc_any.at[:, column], acc_scr.at[step], in_sem.at[step, 0]),
                pltpu.make_async_copy(stat_any.at[step], stat_scr.at[step], in_sem.at[step, 1]),
            )

        def out_copy(step):
            column = pl.ds(pl.multiple_of(step * step_width, step_width), step_width)
            return pltpu.make_async_copy(out_scr.at[step], out_any.at[:, column], out_sem.at[step])

        lax.fori_loop(0, REQ_DEV * PREF, start_kv, 0, unroll=8)
        for copy in in_copies(0):
            copy.start()
        v_scr[:, :, HD:] = jnp.ones((REQ_DEV, keys, HD), v_scr.dtype)
        lax.fori_loop(0, REQ_DEV * PREF, wait_kv, 0, unroll=8)
        v_scr[:, :, :HD] = kv_scr[:, :, HD:]

        def attend(step, with_maximum):
            for part in range(HEAD_STEP):
                column = slice(part * HD, (part + 1) * HD)
                q_column = pl.ds(pl.multiple_of((step * HEAD_STEP + part) * HD, HD), HD)
                for slot in range(slots):
                    owner = owner_ref[slot]
                    live = count_ref[owner] * PB
                    for first in range(slot * span, (slot + 1) * span, ROW_TILE):
                        tile = slice(first, first + ROW_TILE)
                        s = scores_of(q_ref[tile, q_column], kv_scr[owner, :, :HD])
                        key = sure + lax.broadcasted_iota(jnp.int32, (ROW_TILE, keys - sure), 1)
                        s = jnp.concatenate([s[:, :sure], jnp.where(key < live, s[:, sure:], MASKED)], axis=1)
                        top = stat_scr[step, tile, 2 * part : 2 * part + 1]
                        total = stat_scr[step, tile, 2 * part + 1 : 2 * part + 2]
                        total_acc = acc_scr[step, tile, column]
                        if with_maximum:
                            old_top = top
                            top = jnp.maximum(old_top, jnp.max(s, axis=1, keepdims=True))
                            keep = jnp.exp2((old_top - top) * EXP_SCALE)
                            total, total_acc = total * keep, total_acc * keep
                        p = jnp.exp2((s - top) * EXP_SCALE).astype(jnp.bfloat16)
                        o = jnp.dot(p, v_scr[owner], preferred_element_type=jnp.float32)
                        result = (total_acc + o[:, :HD]) / (total + o[:, HD:])
                        out_scr[step, tile, column] = result.astype(out_scr.dtype)

        def one_step(step, carry):
            @pl.when(step + 1 < steps)
            def _():
                for copy in in_copies(step + 1):
                    copy.start()

            for copy in in_copies(step):
                copy.wait()
            bounded = excess_ref[step] < EXP2_LIMIT

            @pl.when(bounded)
            def _():
                attend(step, False)

            @pl.when(jnp.logical_not(bounded))
            def _():
                attend(step, True)

            out_copy(step).start()
            return carry

        lax.fori_loop(0, steps, one_step, 0)
        for step in range(steps):
            out_copy(step).wait()

    smem, anywhere = pl.BlockSpec(memory_space=pltpu.SMEM), pl.BlockSpec(memory_space=pl.ANY)
    return pl.pallas_call(
        kernel,
        in_specs=[smem] * 4 + [pl.BlockSpec(memory_space=pltpu.VMEM)] + [anywhere] * 3,
        out_specs=anywhere,
        scratch_shapes=[
            pltpu.VMEM((REQ_DEV, keys, 2 * HD), jnp.bfloat16),
            pltpu.VMEM((REQ_DEV, keys, 2 * HD), jnp.bfloat16),
            pltpu.VMEM((steps, rows, step_width), jnp.float32),
            pltpu.VMEM((steps, rows, HD), jnp.float32),
            pltpu.VMEM((steps, rows, step_width), jnp.bfloat16),
            pltpu.SemaphoreType.DMA((REQ_DEV * PREF,)),
            pltpu.SemaphoreType.DMA((steps, 2)),
            pltpu.SemaphoreType.DMA((steps,)),
        ],
        out_shape=jax.ShapeDtypeStruct((rows, width), jnp.bfloat16),
        compiler_params=pltpu.CompilerParams(vmem_limit_bytes=PREFIX_VMEM_LIMIT),
        cost_estimate=pl.CostEstimate(
            flops=4 * rows * keys * width, bytes_accessed=12 * rows * width, transcendentals=rows * keys * width // HD
        ),
        name="prefix_attention",
    )(slot_request, places, prefix_count, excess, queries, received, acc, stat)


def used_rows(prefix_ids, prefix_count, block_row):
    known = jnp.arange(block_row.shape[0], dtype=jnp.int32)
    ids = prefix_ids.reshape(-1)
    rows = jnp.sum(jnp.where(ids[:, None] == known, block_row, 0), axis=-1)
    live = (jnp.arange(PREF, dtype=jnp.int32)[None, :] < prefix_count[:, None]).reshape(-1)
    return jnp.where(live, rows, -1)


def share_over_req(values):
    groups = lax.axis_size("req")
    known = values[None, :]
    for steps in ((1,), (2, 4, 6), (8, 16, 24)):
        parts = [lax.ppermute(known, "req", [(d, d ^ step) for d in range(groups)]) for step in steps]
        known = jnp.concatenate([known] + parts, axis=0)
    return known


def low_high(rows, first_row, group_rows):
    within = rows - first_row
    member = (within >= 0) & (within < group_rows)
    low = jnp.min(jnp.where(member, within, group_rows), axis=-1)
    high = jnp.max(jnp.where(member, within, 0), axis=-1)
    return jnp.minimum(low, high), high


def on_device(queries, new_kv, pool_kv, slot_request, prefix_ids, prefix_count, block_row):
    tp_count = lax.axis_size("tp")
    groups = lax.axis_size("req")
    me = lax.axis_index("req").astype(jnp.int32)
    pool_local = pool_kv.shape[0]
    head_width = pool_kv.shape[2] // tp_count
    group_rows = tp_count * pool_local
    rows = used_rows(prefix_ids, prefix_count, block_row)
    low, high = low_high(share_over_req(rows), me * group_rows, group_rows)
    wanted = jnp.stack([low, high], axis=1).reshape(-1)
    by_head = lay_by_head(pool_kv, head_width)
    group_store = lax.all_to_all(by_head, "tp", split_axis=0, concat_axis=0, tiled=True)
    group_store = group_store.reshape(group_rows, PB, head_width)
    to_send = pick_blocks(wanted, me[None], group_store)
    received = lax.all_to_all(to_send, "req", split_axis=0, concat_axis=0, tiled=True)
    same_group = rows[:, None] // group_rows == rows[None, :] // group_rows
    is_high = jnp.any(same_group & (rows[None, :] < rows[:, None]) & (rows[None, :] >= 0), axis=1)
    places = jnp.where(rows >= 0, SLOT_CAP * (rows // group_rows) + is_high.astype(jnp.int32), 0)
    acc, stat, excess = fresh_attention(queries, new_kv, slot_request)
    return prefix_attention(queries, received, acc, stat, excess, slot_request, places, prefix_count)


def solution(mesh):
    return jax.shard_map(
        on_device,
        mesh=mesh,
        in_specs=(
            P("req", "tp"),
            P("req", "tp"),
            P(("req", "tp"), None, None),
            P("req"),
            P("req", None),
            P("req"),
            P(),
        ),
        out_specs=P("req", "tp"),
        check_vma=False,
    )
```
